256 devices in a mesh: col: 4 (over z_hi), row: 64 (over x, z_lo, y, core).
Axes of the slice: x: 4, y: 4, z: 8 (z_hi: 4, z_lo: 2; z = z_hi * 2 + z_lo), core: 2. Of those that a mesh axis runs over, the one named last changes fastest.
Arguments:
- tokens: bfloat16 [128, 16384], P(None, 'row'), may hold values from -6 to 6
- output_gradient: bfloat16 [128, 16384], P(None, 'row'), may hold values from -3 to 3
- gate_values: bfloat16 [16384, 26624], P('row', 'col'), may hold values from -0.125 to 0.125
- gate_scales: float32 [128, 208], P('row', 'col'), may hold values from 0.5 to 2
- up_values: bfloat16 [16384, 26624], P('row', 'col'), may hold values from -0.125 to 0.125
- up_scales: float32 [128, 208], P('row', 'col'), may hold values from 0.5 to 2
- down_values: bfloat16 [26624, 16384], P('col', 'row'), may hold values from -0.109375 to 0.109375
- down_scales: float32 [208, 128], P('col', 'row'), may hold values from 0.5 to 2
- gate_reduce_factor: bfloat16 [64, 16384], P(None, 'row'), may hold values from -0.09375 to 0.09375
- gate_expand: bfloat16 [64, 26624], P(None, ('col', 'row')), may hold values from -0.09375 to 0.09375
- up_reduce_factor: bfloat16 [64, 16384], P(None, 'row'), may hold values from -0.09375 to 0.09375
- up_expand: bfloat16 [64, 26624], P(None, ('col', 'row')), may hold values from -0.09375 to 0.09375
- down_reduce: bfloat16 [64, 26624], P(None, ('col', 'row')), may hold values from -0.09375 to 0.09375
- down_expand: bfloat16 [64, 16384], P(None, 'row'), may hold values from -0.046875 to 0.046875
Outputs:
- input_gradient: bfloat16 [128, 16384], P('col', 'row')
- gate_reduce_gradient: float32 [64, 16384], P(None, 'row')
- gate_expand_gradient: float32 [64, 26624], P(None, ('col', 'row'))
- up_reduce_gradient: float32 [64, 16384], P(None, 'row')
- up_expand_gradient: float32 [64, 26624], P(None, ('col', 'row'))
- down_reduce_gradient: float32 [64, 26624], P(None, ('col', 'row'))
- down_expand_gradient: float32 [64, 16384], P(None, 'row')
The draws below stay inside these ranges and needn't reach their ends.
All inputs are finite; a program needn't handle non-finite values.
Results may differ from the reference program's by a relative error of at most 0.017.
Values may be sent and summed in bfloat16 or wider, within the bound.
No kernel may reach another device: no remote copies, remote signals or barrier semaphores. Data moves between devices by JAX's collectives and lax.ppermute only.
A program may use at most 128 MiB of HBM per device.

```python
import math
import jax
import jax.numpy as jnp
from jax import lax

D = 16384
FF = 26624
R = 64
BLOCK = 128
TOKENS = 128
N_COL = 4


def with_spikes(entries, rng, source, target, shards_of, factor):
    owner, partner = [(jnp.arange(entries.shape[axis_at]) // (entries.shape[axis_at] // shards_of)).reshape([-1 if axis == axis_at else 1 for axis in range(entries.ndim)]) for axis_at in (source, target)]
    chosen = jax.random.permutation(rng, shards_of)[partner]
    strong = (owner == chosen) | (owner == (partner + shards_of // 2) % shards_of)
    return jnp.where(strong, factor * entries, entries)


def levels(rng, dims, cuts, least, high):
    def one(position, parts):
        heights = jax.random.uniform(jax.random.fold_in(jax.random.fold_in(rng, 6), position), (parts,), jnp.float32, least / len(cuts), high / len(cuts))
        return jnp.repeat(jnp.exp(heights), dims[position] // parts).reshape((-1,) + (1,) * (len(dims) - position - 1))

    level = one(*cuts[0])
    for cut in cuts[1:]:
        level = level * one(*cut)
    return level


def normal_values(own_key, extent, spread, limit, shards=(), held_as=jnp.bfloat16):
    gain = levels(own_key, extent, shards, -0.22, 0.18) if shards else 1.0
    values = jax.random.normal(own_key, extent, jnp.float32) * spread * gain
    return jnp.minimum(jnp.maximum(values, -limit), limit).astype(held_as)


def gaussian_with(own_key, dims, deviation, bound, cuts, heavy, kind=jnp.bfloat16):
    drawn = deviation * jax.random.normal(own_key, dims, jnp.float32)
    if cuts:
        drawn = drawn * levels(own_key, dims, cuts, -0.22, 0.18)
    return jnp.clip(with_spikes(drawn, jax.random.fold_in(own_key, 3), *heavy), -bound, bound).astype(kind)


def setup_inputs(seed: int = 0) -> dict:
    splits = jax.random.split(jax.random.key(seed), 15)
    return {
        "tokens": normal_values(splits[0], (TOKENS, D), 1.0, 6.0, ((1, 64),)),
        "output_gradient": normal_values(splits[1], (TOKENS, D), 0.5, 3.0, ((1, 64),)),
        "gate_values": gaussian_with(splits[2], (D, FF), D ** -0.5, 0.125, ((0, 64), (1, 4)), (0, 1, 64, 4.0)),
        "gate_scales": jnp.clip(jnp.exp(math.log(2.0) - 1.3862944 * jax.random.uniform(splits[3], (D // BLOCK, FF // BLOCK), jnp.float32) ** levels(splits[3], (D // BLOCK, FF // BLOCK), ((0, 64), (1, 4)), -0.2, 0.2)), 0.5, 2.0),
        "up_values": gaussian_with(splits[4], (D, FF), D ** -0.5, 0.125, ((0, 64), (1, 4)), (0, 1, 64, 4.0)),
        "up_scales": jnp.clip(jnp.exp(math.log(2.0) - 1.3862944 * jax.random.uniform(splits[5], (D // BLOCK, FF // BLOCK), jnp.float32) ** levels(splits[5], (D // BLOCK, FF // BLOCK), ((0, 64), (1, 4)), -0.2, 0.2)), 0.5, 2.0),
        "down_values": gaussian_with(splits[6], (FF, D), FF ** -0.5, 0.109375, ((0, 4), (1, 64)), (1, 0, 64, 4.0)),
        "down_scales": jnp.clip(jnp.exp(math.log(2.0) - 1.3862944 * jax.random.uniform(splits[7], (FF // BLOCK, D // BLOCK), jnp.float32) ** levels(splits[7], (FF // BLOCK, D // BLOCK), ((0, 4), (1, 64)), -0.2, 0.2)), 0.5, 2.0),
        "gate_reduce_factor": normal_values(splits[8], (R, D), (D // 4) ** -0.5, 0.09375, ((1, 64),)),
        "gate_expand": normal_values(splits[9], (R, FF), (64 * R) ** -0.5, 0.09375, ((1, 256),)),
        "up_reduce_factor": normal_values(splits[10], (R, D), (D // 4) ** -0.5, 0.09375, ((1, 64),)),
        "up_expand": normal_values(splits[11], (R, FF), (64 * R) ** -0.5, 0.09375, ((1, 256),)),
        "down_reduce": normal_values(splits[12], (R, FF), (64 * R) ** -0.5, 0.09375, ((1, 256),)),
        "down_expand": normal_values(splits[13], (R, D), D ** -0.5, 0.046875, ((1, 64),)),
    }


adapter_scale = 0.5


def dequantize(values, scales):
    height, breadth = values.shape
    blocks = values.astype(jnp.float32).reshape(height // BLOCK, BLOCK, breadth // BLOCK, BLOCK)
    return (blocks * scales[:, None, :, None]).reshape(height, breadth).astype(jnp.bfloat16)


def matrix_multiply(left, right):
    return jnp.dot(left, right, preferred_element_type=jnp.float32)


def reference(tokens, output_gradient, gate_values, gate_scales, up_values, up_scales, down_values, down_scales, gate_reduce_factor, gate_expand, up_reduce_factor, up_expand, down_reduce, down_expand):
    gate_lowrank = matrix_multiply(tokens, gate_reduce_factor.T).astype(jnp.bfloat16)
    up_lowrank = matrix_multiply(tokens, up_reduce_factor.T).astype(jnp.bfloat16)
    down_lowrank = matrix_multiply(output_gradient, down_expand.T).astype(jnp.bfloat16)
    width = FF // N_COL
    scale_width = width // BLOCK

    def block_step(carry, index):
        start = (index * width).astype(jnp.int32)
        scale_start = (index * scale_width).astype(jnp.int32)
        gate_weight = dequantize(lax.dynamic_slice_in_dim(gate_values, start, width, 1), lax.dynamic_slice_in_dim(gate_scales, scale_start, scale_width, 1))
        up_weight = dequantize(lax.dynamic_slice_in_dim(up_values, start, width, 1), lax.dynamic_slice_in_dim(up_scales, scale_start, scale_width, 1))
        down_weight = dequantize(lax.dynamic_slice_in_dim(down_values, start, width, 0), lax.dynamic_slice_in_dim(down_scales, scale_start, scale_width, 0))
        gate_exponent = lax.dynamic_slice_in_dim(gate_expand, start, width, 1)
        up_exponent = lax.dynamic_slice_in_dim(up_expand, start, width, 1)
        down_rank_product = lax.dynamic_slice_in_dim(down_reduce, start, width, 1)
        gate_preact = matrix_multiply(tokens, gate_weight) + adapter_scale * matrix_multiply(gate_lowrank, gate_exponent)
        upper_preact = matrix_multiply(tokens, up_weight) + adapter_scale * matrix_multiply(up_lowrank, up_exponent)
        backward_result = matrix_multiply(output_gradient, down_weight.T) + adapter_scale * matrix_multiply(down_lowrank, down_rank_product)
        sigma = jax.nn.sigmoid(gate_preact)
        activated = gate_preact * sigma
        hidden_state = (activated * upper_preact).astype(jnp.bfloat16)
        gate_gradient = (backward_result * upper_preact * sigma * (1.0 + gate_preact * (1.0 - sigma))).astype(jnp.bfloat16)
        upper_gradient = (backward_result * activated).astype(jnp.bfloat16)
        input_portion, gate_part, up_part, hidden_part = carry
        input_portion = input_portion + matrix_multiply(gate_gradient, gate_weight.T) + matrix_multiply(upper_gradient, up_weight.T)
        gate_part = gate_part + matrix_multiply(gate_gradient, gate_exponent.T)
        up_part = up_part + matrix_multiply(upper_gradient, up_exponent.T)
        hidden_part = hidden_part + matrix_multiply(hidden_state, down_rank_product.T)
        partial_pieces = (adapter_scale * matrix_multiply(gate_lowrank.T, gate_gradient), adapter_scale * matrix_multiply(up_lowrank.T, upper_gradient), adapter_scale * matrix_multiply(down_lowrank.T, hidden_state))
        return (input_portion, gate_part, up_part, hidden_part), partial_pieces

    start_carry = (jnp.zeros((TOKENS, D), jnp.float32), jnp.zeros((TOKENS, R), jnp.float32), jnp.zeros((TOKENS, R), jnp.float32), jnp.zeros((TOKENS, R), jnp.float32))
    carry, partial_pieces = lax.scan(block_step, start_carry, jnp.arange(N_COL, dtype=jnp.int32))
    input_portion, gate_part, up_part, hidden_part = carry
    gate_total_sum = gate_part.astype(jnp.bfloat16)
    up_total_sum = up_part.astype(jnp.bfloat16)
    hidden_total_sum = hidden_part.astype(jnp.bfloat16)
    input_gradient = (input_portion + adapter_scale * (matrix_multiply(gate_total_sum, gate_reduce_factor) + matrix_multiply(up_total_sum, up_reduce_factor))).astype(jnp.bfloat16)
    gate_reduce_gradient = adapter_scale * matrix_multiply(gate_total_sum.T, tokens)
    up_reduce_gradient = adapter_scale * matrix_multiply(up_total_sum.T, tokens)
    down_expand_gradient = adapter_scale * matrix_multiply(hidden_total_sum.T, output_gradient)

    def joined(stacked):
        return jnp.transpose(stacked, (1, 0, 2)).reshape(R, FF)

    return (input_gradient, gate_reduce_gradient, joined(partial_pieces[0]), up_reduce_gradient, joined(partial_pieces[1]), joined(partial_pieces[2]), down_expand_gradient)
```

```python
import functools

import jax
import jax.numpy as jnp
from jax import lax
from jax.experimental import pallas as pl
from jax.experimental.pallas import tpu as pltpu
from jax.sharding import PartitionSpec as P

BLOCK = 128
SCALE = 0.5
STEPS = 4
BF16 = jnp.bfloat16
F32 = jnp.float32
LIMIT = 24 * 1024 * 1024


def params():
    return pltpu.CompilerParams(vmem_limit_bytes=LIMIT)


def dot(left, right, left_dim, right_dim):
    return lax.dot_general(
        left, right, (((left_dim,), (right_dim,)), ((), ())), preferred_element_type=F32
    )


def whole(shape):
    return pl.BlockSpec(shape, lambda *_: (0,) * len(shape))


def smem():
    return pl.BlockSpec(memory_space=pltpu.SMEM)


def dequantize_wide(values_ref, scales_ref, first, weight_ref):
    for block in range(values_ref.shape[1] // BLOCK):
        columns = pl.ds(block * BLOCK, BLOCK)
        for part in range(values_ref.shape[0] // BLOCK):
            rows = pl.ds(part * BLOCK, BLOCK)
            scale = scales_ref[part, first + block]
            weight_ref[rows, columns] = (values_ref[rows, columns].astype(F32) * scale).astype(BF16)


def dequantize_tall(values_ref, scales_ref, first, weight_ref):
    for block in range(values_ref.shape[0] // BLOCK):
        rows = pl.ds(block * BLOCK, BLOCK)
        for part in range(values_ref.shape[1] // BLOCK):
            columns = pl.ds(part * BLOCK, BLOCK)
            scale = scales_ref[first + block, part]
            weight_ref[rows, columns] = (values_ref[rows, columns].astype(F32) * scale).astype(BF16)


def partial_kernel(tall, where_ref, scales_ref, inputs_ref, values_ref, send_ref, keep_ref, weight_ref, sums_ref):
    core = where_ref[0]
    blocks = weight_ref.shape[0 if tall else 1] // BLOCK
    first = pl.program_id(0) * blocks
    if tall:
        dequantize_tall(values_ref, scales_ref, first, weight_ref)
        sums_ref[...] = dot(weight_ref[...], inputs_ref[...], 1, 1)
    else:
        dequantize_wide(values_ref, scales_ref, first, weight_ref)
        product = dot(inputs_ref[...], weight_ref[...], 1, 0)
        sums_ref[...] = product.T
    chips, piece = send_ref.shape[:2]
    for chip in range(chips):
        start = chip * 2 * piece
        mine = pl.multiple_of(start + core * piece, 8)
        theirs = pl.multiple_of(start + (1 - core) * piece, 8)
        keep_ref[chip] = sums_ref[pl.ds(mine, piece), :].astype(BF16)
        send_ref[chip] = sums_ref[pl.ds(theirs, piece), :].astype(BF16)


def partial_sums(tall, where, scales, inputs, values, piece):
    hidden = values.shape[0 if tall else 1]
    width = values.shape[1 if tall else 0]
    part = hidden // STEPS
    chips = hidden // (2 * piece)
    tokens = inputs.shape[0]
    out = jax.ShapeDtypeStruct((chips, piece, tokens), BF16)
    block = pl.BlockSpec((chips // STEPS, piece, tokens), lambda i: (i, 0, 0))
    values_block = (
        pl.BlockSpec((part, width), lambda i: (i, 0))
        if tall
        else pl.BlockSpec((width, part), lambda i: (0, i))
    )
    return pl.pallas_call(
        functools.partial(partial_kernel, tall),
        grid=(STEPS,),
        in_specs=[smem(), smem(), whole(inputs.shape), values_block],
        out_specs=[block, block],
        out_shape=[out, out],
        scratch_shapes=[
            pltpu.VMEM((part, width) if tall else (width, part), BF16),
            pltpu.VMEM((part, tokens), F32),
        ],
        compiler_params=params(),
        cost_estimate=pl.CostEstimate(
            flops=2 * tokens * width * hidden, bytes_accessed=2 * width * hidden, transcendentals=0
        ),
    )(where, scales, inputs, values)


def low_kernel(where_ref, tokens_ref, gradient_ref, gate_ref, up_ref, down_ref, send_ref, keep_ref, low_ref):
    core = where_ref[0]
    half = low_ref.shape[1] // 2
    low_ref[0] = dot(gate_ref[...], tokens_ref[...], 1, 1)
    low_ref[1] = dot(up_ref[...], tokens_ref[...], 1, 1)
    low_ref[2] = dot(down_ref[...], gradient_ref[...], 1, 1)
    mine = pl.multiple_of(core * half, half)
    theirs = pl.multiple_of((1 - core) * half, half)
    for kind in range(3):
        keep_ref[kind] = low_ref[kind, pl.ds(mine, half), :].astype(BF16)
        send_ref[kind] = low_ref[kind, pl.ds(theirs, half), :].astype(BF16)


def low_partials(where, tokens, gradient, gate_reduce, up_reduce, down_expand):
    rank, count = gate_reduce.shape[0], tokens.shape[0]
    out = jax.ShapeDtypeStruct((3, rank // 2, count), BF16)
    return pl.pallas_call(
        low_kernel,
        in_specs=[smem()] + [pl.BlockSpec(memory_space=pltpu.VMEM)] * 5,
        out_specs=[pl.BlockSpec(memory_space=pltpu.VMEM)] * 2,
        out_shape=[out, out],
        scratch_shapes=[pltpu.VMEM((3, rank, count), F32)],
        compiler_params=params(),
    )(where, tokens, gradient, gate_reduce, up_reduce, down_expand)


def pack_kernel(*refs):
    keeps, received, out_ref = refs[:4], refs[4:8], refs[8]
    low = (keeps[3][...].astype(F32) + received[3][...].astype(F32)).reshape(-1, out_ref.shape[2])
    for chip in range(out_ref.shape[0]):
        parts = [keeps[k][chip].astype(F32) + received[k][chip].astype(F32) for k in range(3)]
        out_ref[chip] = jnp.concatenate(parts + [low], axis=0).astype(BF16)


def pack(keeps, received):
    chips, piece, tokens = keeps[0].shape
    low_shape = keeps[3].shape
    rows = 3 * piece + low_shape[0] * low_shape[1]
    block = pl.BlockSpec((chips // STEPS, piece, tokens), lambda i: (i, 0, 0))
    specs = [block] * 3 + [whole(low_shape)]
    return pl.pallas_call(
        pack_kernel,
        grid=(STEPS,),
        in_specs=specs + specs,
        out_specs=pl.BlockSpec((chips // STEPS, rows, tokens), lambda i: (i, 0, 0)),
        out_shape=jax.ShapeDtypeStruct((chips, rows, tokens), BF16),
        compiler_params=params(),
    )(*keeps, *received)


def total_kernel(parts_ref, sums_ref, low_ref):
    rows = sums_ref.shape[0]

    def add(first, count):
        total = parts_ref[0, first : first + count].astype(F32)
        for chip in range(1, parts_ref.shape[0]):
            total = total + parts_ref[chip, first : first + count].astype(F32)
        return total

    for first in range(0, rows, 104):
        sums_ref[first : first + 104] = add(first, 104)
    low_ref[...] = add(rows, low_ref.shape[0]).astype(BF16)


def total(parts, rows):
    _, everything, tokens = parts.shape
    return pl.pallas_call(
        total_kernel,
        in_specs=[pl.BlockSpec(memory_space=pltpu.VMEM)],
        out_specs=[pl.BlockSpec(memory_space=pltpu.VMEM)] * 2,
        out_shape=[
            jax.ShapeDtypeStruct((rows, tokens), F32),
            jax.ShapeDtypeStruct((everything - rows, tokens), BF16),
        ],
        compiler_params=params(),
    )(parts)


def middle_kernel(
    where_ref, sums_ref, mine_ref, theirs_ref, gate_expand_ref, up_expand_ref, down_reduce_ref,
    send_ref, keep_ref, gate_out, up_out, down_out, low_ref, rank_ref,
):
    core = where_ref[0]
    piece = gate_expand_ref.shape[1]
    half = low_ref.shape[1] // 2
    mine = pl.multiple_of(core * half, half)
    theirs = pl.multiple_of((1 - core) * half, half)
    for kind in range(3):
        low_ref[kind, pl.ds(mine, half), :] = mine_ref[kind * half : (kind + 1) * half].astype(F32)
        low_ref[kind, pl.ds(theirs, half), :] = theirs_ref[kind * half : (kind + 1) * half].astype(F32)
    expands = [gate_expand_ref[...], up_expand_ref[...], down_reduce_ref[...]]
    lows = [low_ref[kind].astype(BF16) for kind in range(3)]
    gate, upper, back = [
        sums_ref[kind * piece : (kind + 1) * piece] + SCALE * dot(expands[kind], lows[kind], 0, 0)
        for kind in range(3)
    ]
    sigma = jax.nn.sigmoid(gate)
    activated = gate * sigma
    hidden = (activated * upper).astype(BF16)
    grad_gate = (back * upper * sigma * (1.0 + gate * (1.0 - sigma))).astype(BF16)
    grad_upper = (back * activated).astype(BF16)
    gate_out[...] = SCALE * dot(lows[0], grad_gate, 1, 1)
    up_out[...] = SCALE * dot(lows[1], grad_upper, 1, 1)
    down_out[...] = SCALE * dot(lows[2], hidden, 1, 1)
    rank_ref[0] = dot(expands[0], grad_gate, 1, 0)
    rank_ref[1] = dot(expands[1], grad_upper, 1, 0)
    rank_ref[2] = dot(expands[2], hidden, 1, 0)
    first = core == 0
    keep_rows = [jnp.where(first, grad_gate.astype(F32), grad_upper.astype(F32))]
    send_rows = [jnp.where(first, grad_upper.astype(F32), grad_gate.astype(F32))]
    for kind in range(3):
        keep_rows.append(rank_ref[kind, pl.ds(mine, half), :])
        send_rows.append(rank_ref[kind, pl.ds(theirs, half), :])
    keep_ref[...] = jnp.concatenate(keep_rows, axis=0)
    send_ref[...] = jnp.concatenate(send_rows, axis=0).astype(BF16)


def middle(where, sums, mine, theirs, gate_expand, up_expand, down_reduce):
    rank, piece = gate_expand.shape
    tokens = sums.shape[1]
    rows = piece + 3 * rank // 2
    vmem = pl.BlockSpec(memory_space=pltpu.VMEM)
    return pl.pallas_call(
        middle_kernel,
        in_specs=[smem()] + [vmem] * 6,
        out_specs=[vmem] * 5,
        out_shape=[
            jax.ShapeDtypeStruct((rows, tokens), BF16),
            jax.ShapeDtypeStruct((rows, tokens), F32),
        ]
        + [jax.ShapeDtypeStruct((rank, piece), F32)] * 3,
        scratch_shapes=[pltpu.VMEM((3, rank, tokens), F32), pltpu.VMEM((3, rank, tokens), F32)],
        compiler_params=params(),
    )(where, sums, mine, theirs, gate_expand, up_expand, down_reduce)


def spread_kernel(piece, where_ref, keep_ref, received_ref, out_ref):
    first = where_ref[0] == 0
    kept = keep_ref[:piece]
    arrived = received_ref[:piece].astype(F32)
    block = jnp.concatenate(
        [
            jnp.where(first, kept, arrived),
            jnp.where(first, arrived, kept),
            keep_ref[piece:] + received_ref[piece:].astype(F32),
        ],
        axis=0,
    ).astype(BF16)
    for chip in range(out_ref.shape[0]):
        out_ref[chip] = block


def spread(where, keep, received, piece, chips):
    rows, tokens = keep.shape
    vmem = pl.BlockSpec(memory_space=pltpu.VMEM)
    return pl.pallas_call(
        functools.partial(spread_kernel, piece),
        in_specs=[smem(), vmem, vmem],
        out_specs=vmem,
        out_shape=jax.ShapeDtypeStruct((chips, rows + piece, tokens), BF16),
        compiler_params=params(),
    )(where, keep, received)


def back_kernel(last, *refs):
    if last:
        (where_ref, gate_scales, up_scales, grads_ref, gate_ref, up_ref, before_ref, before_rank_ref,
         own_ref, *to_refs, weight_ref, total_ref, rank_ref, turned_ref) = refs
    else:
        (where_ref, gate_scales, up_scales, grads_ref, gate_ref, up_ref,
         total_ref, rank_ref, weight_ref) = refs
    step = pl.program_id(0)
    gate_turn = where_ref[0] == (1 if last else 0)
    blocks = weight_ref.shape[1] // BLOCK
    first = step * blocks
    unit_rows = weight_ref.shape[1] // grads_ref.shape[0]

    @pl.when(gate_turn)
    def _():
        dequantize_wide(gate_ref, gate_scales, first, weight_ref)

    @pl.when(jnp.logical_not(gate_turn))
    def _():
        dequantize_wide(up_ref, up_scales, first, weight_ref)

    grads = jnp.concatenate([grads_ref[chip, :unit_rows] for chip in range(grads_ref.shape[0])], axis=0)
    product = dot(weight_ref[...], grads, 1, 0)
    rank = grads_ref[0, unit_rows:].astype(F32)
    for chip in range(1, grads_ref.shape[0]):
        rank = rank + grads_ref[chip, unit_rows:].astype(F32)

    @pl.when(step == 0)
    def _():
        total_ref[...] = product + before_ref[...] if last else product
        rank_ref[...] = rank

    @pl.when(step > 0)
    def _():
        total_ref[...] += product
        rank_ref[...] += rank

    if last:

        @pl.when(step == pl.num_programs(0) - 1)
        def _():
            core, column = where_ref[0], where_ref[1]
            turned_ref[...] = total_ref[...].T
            half = rank_ref.shape[0] // 3
            mine = [before_rank_ref[k * half : (k + 1) * half] for k in range(3)]
            theirs = [rank_ref[k * half : (k + 1) * half] for k in range(3)]
            rows = []
            for kind in range(3):
                rows.append(jnp.where(core == 0, mine[kind], theirs[kind]))
                rows.append(jnp.where(core == 0, theirs[kind], mine[kind]))
            share = turned_ref.shape[0] // 4
            for offset, out_ref in enumerate([own_ref, *to_refs]):
                start = pl.multiple_of(lax.rem(column + offset, 4) * share, share)
                piece = turned_ref[pl.ds(start, share), :]
                block = jnp.concatenate([piece[:, :BLOCK], piece[:, BLOCK:], *rows], axis=0)
                out_ref[...] = block.astype(BF16)


def back(last, where, gate_scales, up_scales, grads, gate_values, up_values, before=()):
    width, hidden = gate_values.shape
    chips, rows, tokens = grads.shape
    part = hidden // STEPS
    unit_rows = hidden // chips
    rank_rows = rows - unit_rows
    turn = 1 if last else 0
    gate_block = pl.BlockSpec((width, part), lambda i, w, *_: (0, jnp.where(w[0] == turn, i, 0)))
    up_block = pl.BlockSpec((width, part), lambda i, w, *_: (0, jnp.where(w[0] == turn, 0, i)))
    in_specs = [pl.BlockSpec((chips // STEPS, rows, tokens), lambda i, *_: (i, 0, 0)), gate_block, up_block]
    if last:
        in_specs += [whole((width, tokens)), whole((rank_rows, tokens))]
        out_shape = [jax.ShapeDtypeStruct((64 + 2 * rank_rows, tokens), BF16)] * 4
    else:
        out_shape = [
            jax.ShapeDtypeStruct((width, tokens), F32),
            jax.ShapeDtypeStruct((rank_rows, tokens), F32),
        ]
    scratch = [pltpu.VMEM((width, part), BF16)]
    if last:
        scratch += [
            pltpu.VMEM((width, tokens), F32),
            pltpu.VMEM((rank_rows, tokens), F32),
            pltpu.VMEM((tokens, width), F32),
        ]
    return pl.pallas_call(
        functools.partial(back_kernel, last),
        grid_spec=pltpu.PrefetchScalarGridSpec(
            num_scalar_prefetch=3,
            grid=(STEPS,),
            in_specs=in_specs,
            out_specs=[whole(s.shape) for s in out_shape],
            scratch_shapes=scratch,
        ),
        out_shape=out_shape,
        compiler_params=params(),
        cost_estimate=pl.CostEstimate(
            flops=2 * tokens * width * hidden, bytes_accessed=2 * width * hidden, transcendentals=0
        ),
    )(where, gate_scales, up_scales, grads, gate_values, up_values, *before)


def last_kernel(
    where_ref, own_ref, one_ref, two_ref, three_ref, tokens_ref, gradient_ref, gate_reduce_ref, up_reduce_ref,
    input_out, gate_out, up_out, down_out, parts_ref, wide_ref,
):
    column = where_ref[1]
    for offset, ref in enumerate([own_ref, one_ref, two_ref, three_ref]):
        parts_ref[lax.rem(column + 4 - offset, 4)] = ref[...].astype(F32)
    summed = parts_ref[0] + parts_ref[1] + parts_ref[2] + parts_ref[3]
    share = input_out.shape[0]
    rank = gate_out.shape[0]
    sums = [summed[2 * share + k * rank : 2 * share + (k + 1) * rank].astype(BF16) for k in range(3)]
    wide_ref[...] = dot(sums[0], gate_reduce_ref[...], 0, 0) + dot(sums[1], up_reduce_ref[...], 0, 0)
    start = pl.multiple_of(column * share, share)
    main = jnp.concatenate([summed[:share], summed[share : 2 * share]], axis=1)
    input_out[...] = (main + SCALE * wide_ref[pl.ds(start, share), :]).astype(BF16)
    gate_out[...] = SCALE * dot(sums[0], tokens_ref[...], 1, 0)
    up_out[...] = SCALE * dot(sums[1], tokens_ref[...], 1, 0)
    down_out[...] = SCALE * dot(sums[2], gradient_ref[...], 1, 0)


def finish(where, own, others, tokens, gradient, gate_reduce, up_reduce):
    rank, width = gate_reduce.shape
    count = tokens.shape[0]
    vmem = pl.BlockSpec(memory_space=pltpu.VMEM)
    return pl.pallas_call(
        last_kernel,
        in_specs=[smem()] + [vmem] * 8,
        out_specs=[vmem] * 4,
        out_shape=[jax.ShapeDtypeStruct((count // 4, width), BF16)]
        + [jax.ShapeDtypeStruct((rank, width), F32)] * 3,
        scratch_shapes=[pltpu.VMEM((4,) + own.shape, F32), pltpu.VMEM((count, width), F32)],
        compiler_params=params(),
    )(where, own, *others, tokens, gradient, gate_reduce, up_reduce)


def per_device(
    tokens,
    output_gradient,
    gate_values,
    gate_scales,
    up_values,
    up_scales,
    down_values,
    down_scales,
    gate_reduce_factor,
    gate_expand,
    up_reduce_factor,
    up_expand,
    down_reduce,
    down_expand,
):
    piece = gate_expand.shape[1]
    n_row = lax.axis_size("row")
    chips = n_row // 2
    position = lax.axis_index("row")
    where = jnp.stack([position % 2, lax.axis_index("col")]).astype(jnp.int32)
    swap = [(i, i ^ 1) for i in range(n_row)]
    same_core = [[2 * i + core for i in range(chips)] for core in range(2)]

    def exchange(value):
        return lax.ppermute(value, "row", swap)

    def across_chips(value):
        return lax.all_to_all(value, "row", 0, 0, tiled=True, axis_index_groups=same_core)

    sends = [
        partial_sums(False, where, gate_scales, tokens, gate_values, piece),
        partial_sums(False, where, up_scales, tokens, up_values, piece),
        partial_sums(True, where, down_scales, output_gradient, down_values, piece),
        low_partials(where, tokens, output_gradient, gate_reduce_factor, up_reduce_factor, down_expand),
    ]
    received = [exchange(send) for send, _ in sends]
    parts = across_chips(pack([keep for _, keep in sends], received))
    sums, low = total(parts, 3 * piece)
    send, keep, gate_expand_gradient, up_expand_gradient, down_reduce_gradient = middle(
        where, sums, low, exchange(low), gate_expand, up_expand, down_reduce
    )
    mine = across_chips(spread(where, keep, exchange(send), piece, chips))
    theirs = exchange(mine)
    begun = back(False, where, gate_scales, up_scales, mine, gate_values, up_values)
    own, *out = back(True, where, gate_scales, up_scales, theirs, gate_values, up_values, begun)
    others = [
        lax.ppermute(value, "col", [(i, (i + offset) % 4) for i in range(4)])
        for offset, value in zip((1, 2, 3), out)
    ]
    input_gradient, gate_reduce_gradient, up_reduce_gradient, down_expand_gradient = finish(
        where, own, others, tokens, output_gradient, gate_reduce_factor, up_reduce_factor
    )
    return (
        input_gradient,
        gate_reduce_gradient,
        gate_expand_gradient,
        up_reduce_gradient,
        up_expand_gradient,
        down_reduce_gradient,
        down_expand_gradient,
    )


def solution(mesh):
    in_specs = (
        P(None, "row"),
        P(None, "row"),
        P("row", "col"),
        P("row", "col"),
        P("row", "col"),
        P("row", "col"),
        P("col", "row"),
        P("col", "row"),
        P(None, "row"),
        P(None, ("col", "row")),
        P(None, "row"),
        P(None, ("col", "row")),
        P(None, ("col", "row")),
        P(None, "row"),
    )
    out_specs = (
        P("col", "row"),
        P(None, "row"),
        P(None, ("col", "row")),
        P(None, "row"),
        P(None, ("col", "row")),
        P(None, ("col", "row")),
        P(None, "row"),
    )
    return jax.shard_map(
        per_device, mesh=mesh, in_specs=in_specs, out_specs=out_specs, check_vma=False
    )
```

```python
import functools

import jax
import jax.numpy as jnp
from jax import lax
from jax.experimental import pallas as pl
from jax.experimental.pallas import tpu as pltpu
from jax.sharding import PartitionSpec as P

BLOCK = 128
SCALE = 0.5
STEPS = 4
BF16 = jnp.bfloat16
F32 = jnp.float32
LIMIT = 32 * 1024 * 1024
CHUNK = 512
FIRST_PARTS = (1024, 2048, 3584)
LATER_PARTS = (6656,)


def params():
    return pltpu.CompilerParams(vmem_limit_bytes=LIMIT)


def dot(left, right, left_dim, right_dim):
    return lax.dot_general(
        left, right, (((left_dim,), (right_dim,)), ((), ())), preferred_element_type=F32
    )


def whole(shape):
    return pl.BlockSpec(shape, lambda *_: (0,) * len(shape))


def smem():
    return pl.BlockSpec(memory_space=pltpu.SMEM)


def dequantize_wide(values, scales_ref, first):
    columns = []
    for block in range(values.shape[1] // BLOCK):
        columns.append(
            jnp.concatenate(
                [
                    (values[part * BLOCK : (part + 1) * BLOCK, block * BLOCK : (block + 1) * BLOCK].astype(F32)
                     * scales_ref[part, first + block]).astype(BF16)
                    for part in range(values.shape[0] // BLOCK)
                ],
                axis=0,
            )
        )
    return jnp.concatenate(columns, axis=1)


def dequantize_tall(values, scales_ref, first):
    rows = []
    for block in range(values.shape[0] // BLOCK):
        rows.append(
            jnp.concatenate(
                [
                    (values[block * BLOCK : (block + 1) * BLOCK, part * BLOCK : (part + 1) * BLOCK].astype(F32)
                     * scales_ref[part, first + block]).astype(BF16)
                    for part in range(values.shape[1] // BLOCK)
                ],
                axis=1,
            )
        )
    return jnp.concatenate(rows, axis=0)


def split_by_core(core, sums_ref, send_ref, keep_ref):
    chips, piece = send_ref.shape[:2]
    for chip in range(chips):
        start = chip * 2 * piece
        mine = pl.multiple_of(start + core * piece, 8)
        theirs = pl.multiple_of(start + (1 - core) * piece, 8)
        keep_ref[chip] = sums_ref[pl.ds(mine, piece), :].astype(BF16)
        send_ref[chip] = sums_ref[pl.ds(theirs, piece), :].astype(BF16)


def stay(value):
    return pltpu.with_memory_space_constraint(value, pltpu.HBM)


def fetch_all(sources, buffers, sems):
    copies = [pltpu.make_async_copy(s, b, sems.at[i]) for i, (s, b) in enumerate(zip(sources, buffers))]
    for copy in copies:
        copy.start()
    return copies


def start_parts(values_ref, buffer_ref, sems, axis, sizes):
    parts, first = [], 0
    for step, size in enumerate(sizes):
        part = pl.ds(first, size)
        place = (part, slice(None)) if axis == 0 else (slice(None), part)
        copy = pltpu.make_async_copy(values_ref.at[place], buffer_ref.at[place], sems.at[step])
        copy.start()
        parts.append((copy, first, size))
        first += size
    return parts


def wide_kernel(
    where_ref, gate_scales_hbm, up_scales_hbm, tokens_hbm, gradient_hbm, gate_reduce_hbm, up_reduce_hbm,
    down_expand_hbm, gate_hbm, up_hbm, gate_send, gate_keep, up_send, up_keep, low_ref,
    gate_scales, up_scales, tokens_ref, gradient_ref, gate_reduce_ref, up_reduce_ref, down_expand_ref, gate_ref, up_ref, sums_ref, small, sems,
):
    small_copies = fetch_all(
        [gate_scales_hbm, tokens_hbm, up_scales_hbm, gradient_hbm, gate_reduce_hbm, up_reduce_hbm, down_expand_hbm],
        [gate_scales, tokens_ref, up_scales, gradient_ref, gate_reduce_ref, up_reduce_ref, down_expand_ref],
        small,
    )
    gate_parts = start_parts(gate_hbm, gate_ref, sems.at[0], 1, FIRST_PARTS)
    up_parts = start_parts(up_hbm, up_ref, sems.at[1], 1, LATER_PARTS)
    for copy in small_copies[:3]:
        copy.wait()
    for parts, values_ref, scales_ref, send_ref, keep_ref in (
        (gate_parts, gate_ref, gate_scales, gate_send, gate_keep),
        (up_parts, up_ref, up_scales, up_send, up_keep),
    ):
        for copy, first, size in parts:
            copy.wait()
            for start in range(first, first + size, CHUNK):
                part = slice(start, start + CHUNK)
                weight = dequantize_wide(values_ref[:, part], scales_ref, start // BLOCK)
                sums_ref[part] = dot(tokens_ref[...], weight, 1, 0).T
        split_by_core(where_ref[0], sums_ref, send_ref, keep_ref)
    for copy in small_copies[3:]:
        copy.wait()
    rank = gate_reduce_ref.shape[0]
    low_ref[:rank] = dot(gate_reduce_ref[...], tokens_ref[...], 1, 1).astype(BF16)
    low_ref[rank : 2 * rank] = dot(up_reduce_ref[...], tokens_ref[...], 1, 1).astype(BF16)
    low_ref[2 * rank :] = dot(down_expand_ref[...], gradient_ref[...], 1, 1).astype(BF16)


def tall_kernel(
    where_ref, scales_hbm, gradient_hbm, values_hbm, after_ref, send_ref, keep_ref,
    scales_ref, gradient_ref, values_ref, sums_ref, small, sems,
):
    small_copies = fetch_all([scales_hbm, gradient_hbm], [scales_ref, gradient_ref], small)
    parts = start_parts(values_hbm, values_ref, sems, 0, FIRST_PARTS)
    for copy in small_copies:
        copy.wait()
    for copy, first, size in parts:
        copy.wait()
        for start in range(first, first + size, CHUNK):
            part = slice(start, start + CHUNK)
            weight = dequantize_tall(values_ref[part], scales_ref, start // BLOCK)
            sums_ref[part] = dot(weight, gradient_ref[...], 1, 1)
    split_by_core(where_ref[0], sums_ref, send_ref, keep_ref)


def wide_sums(where, gate_scales, up_scales, tokens, gradient, gate_reduce, up_reduce, down_expand, gate, up, piece):
    width, hidden = gate.shape
    chips, count = hidden // (2 * piece), tokens.shape[0]
    vmem, hbm = pl.BlockSpec(memory_space=pltpu.VMEM), pl.BlockSpec(memory_space=pltpu.HBM)
    fetched = (tokens, gradient, gate_reduce, up_reduce, down_expand, gate, up)
    return pl.pallas_call(
        wide_kernel,
        in_specs=[smem()] + [hbm] * 9,
        out_specs=[vmem] * 5,
        out_shape=[jax.ShapeDtypeStruct((chips, piece, count), BF16)] * 4
        + [jax.ShapeDtypeStruct((3 * gate_reduce.shape[0], count), BF16)],
        scratch_shapes=[pltpu.SMEM(gate_scales.shape, F32)] * 2
        + [pltpu.VMEM(value.shape, BF16) for value in fetched]
        + [
            pltpu.VMEM((hidden, count), F32),
            pltpu.SemaphoreType.DMA((7,)),
            pltpu.SemaphoreType.DMA((2, len(FIRST_PARTS))),
        ],
        compiler_params=params(),
    )(where, *[stay(value) for value in (gate_scales, up_scales, *fetched)])


def tall_sums(where, scales, gradient, values, piece, after):
    hidden, width = values.shape
    chips, count = hidden // (2 * piece), gradient.shape[0]
    vmem, hbm = pl.BlockSpec(memory_space=pltpu.VMEM), pl.BlockSpec(memory_space=pltpu.HBM)
    return pl.pallas_call(
        tall_kernel,
        in_specs=[smem(), hbm, hbm, hbm, pl.BlockSpec(memory_space=pl.ANY)],
        out_specs=[vmem] * 2,
        out_shape=[jax.ShapeDtypeStruct((chips, piece, count), BF16)] * 2,
        scratch_shapes=[
            pltpu.SMEM(scales.shape, F32),
            pltpu.VMEM(gradient.shape, BF16),
            pltpu.VMEM(values.shape, BF16),
            pltpu.VMEM((hidden, count), F32),
            pltpu.SemaphoreType.DMA((2,)),
            pltpu.SemaphoreType.DMA((len(FIRST_PARTS),)),
        ],
        compiler_params=params(),
    )(where, stay(scales), stay(gradient), stay(values), after)


def weights_kernel(gate_scales, up_scales, gate_ref, up_ref, after_ref, gate_out, up_out):
    first = pl.program_id(0) * (gate_ref.shape[1] // BLOCK)
    gate_out[...] = dequantize_wide(gate_ref[...], gate_scales, first)
    up_out[...] = dequantize_wide(up_ref[...], up_scales, first)


def weights(gate_scales, up_scales, gate, up, after):
    width, hidden = gate.shape
    block = pl.BlockSpec((width, hidden // STEPS), lambda i: (0, i))
    return pl.pallas_call(
        weights_kernel,
        grid=(STEPS,),
        in_specs=[smem(), smem(), block, block, pl.BlockSpec(memory_space=pl.ANY)],
        out_specs=[block] * 2,
        out_shape=[jax.ShapeDtypeStruct(gate.shape, BF16)] * 2,
        compiler_params=params(),
        cost_estimate=pl.CostEstimate(
            flops=2 * width * hidden, bytes_accessed=8 * width * hidden, transcendentals=0
        ),
    )(gate_scales, up_scales, gate, up, after)


def vmem_call(kernel, out_shape, *args, scratch=(), unread=0):
    vmem = pl.BlockSpec(memory_space=pltpu.VMEM)
    return pl.pallas_call(
        kernel,
        in_specs=[smem()] + [vmem] * (len(args) - 1 - unread) + [pl.BlockSpec(memory_space=pl.ANY)] * unread,
        out_specs=[vmem] * len(out_shape),
        out_shape=out_shape,
        scratch_shapes=scratch,
        compiler_params=params(),
    )(*args)


def chip_of(core, first, z, second):
    return jnp.where(core == 0, first * 8 + z * 4 + second, second * 8 + z * 4 + first)


def pack_kernel(where_ref, *refs):
    keeps, received, outs = refs[:4], refs[4:8], refs[8:]
    core, first, second = where_ref[0], where_ref[3], where_ref[4]
    low = keeps[3][...].astype(F32) + received[3][...].astype(F32)
    pair = 6 * keeps[0].shape[1]
    for offset, out_ref in enumerate(outs):
        there = lax.rem(first + offset, 4)
        for step in range(4):
            parts = []
            for near in range(2):
                chip = chip_of(core, there, near, lax.rem(second + step, 4))
                parts += [keeps[k][chip].astype(F32) + received[k][chip].astype(F32) for k in range(3)]
            out_ref[step * pair : (step + 1) * pair] = jnp.concatenate(parts, axis=0).astype(out_ref.dtype)
        out_ref[4 * pair :] = low.astype(out_ref.dtype)


def pack(where, keeps, received):
    _, piece, tokens = keeps[0].shape
    rows = 24 * piece + keeps[3].shape[0]
    out_shape = [jax.ShapeDtypeStruct((rows, tokens), F32 if i == 0 else BF16) for i in range(4)]
    return vmem_call(pack_kernel, out_shape, where, *keeps, *received)


def second_kernel(where_ref, own_ref, one_ref, two_ref, three_ref, gate_ref, up_ref, *outs):
    pair = (own_ref.shape[0] - outs[0].shape[0]) // 3

    def add(first, count):
        rows = slice(first, first + count)
        arrived = one_ref[rows].astype(F32) + two_ref[rows].astype(F32) + three_ref[rows].astype(F32)
        return own_ref[rows] + arrived

    low = add(4 * pair, own_ref.shape[0] - 4 * pair)
    for step, out_ref in enumerate(outs):
        out_ref[:pair] = add(step * pair, pair).astype(out_ref.dtype)
        out_ref[pair:] = low.astype(out_ref.dtype)


def second(where, own, arrived, piece, ready):
    rows, tokens = own.shape
    rows -= 18 * piece
    out_shape = [jax.ShapeDtypeStruct((rows, tokens), F32 if i == 0 else BF16) for i in range(4)]
    return vmem_call(second_kernel, out_shape, where, own, *arrived, *ready, unread=2)


def third_kernel(
    where_ref, own_ref, one_ref, two_ref, three_ref, gate_expand_ref, up_expand_ref, down_reduce_ref, keep_ref, send_ref
):
    rows, count = keep_ref.shape
    arrived = one_ref[...].astype(F32) + two_ref[...].astype(F32) + three_ref[...].astype(F32)
    everything = own_ref[...] + arrived
    keep_ref[...] = everything
    send_ref[:rows] = everything.astype(BF16)
    rank, piece = gate_expand_ref.shape
    for kind, ref in enumerate((gate_expand_ref, up_expand_ref, down_reduce_ref)):
        place = slice(rows + kind * rank, rows + (kind + 1) * rank)
        send_ref[place, :piece] = ref[...]
        send_ref[place, piece:] = jnp.zeros((rank, count - piece), BF16)


def third(where, own, arrived, expands):
    rows, count = own.shape
    far_rows = rows + 3 * expands[0].shape[0]
    out_shape = [jax.ShapeDtypeStruct(own.shape, F32), jax.ShapeDtypeStruct((far_rows, count), BF16)]
    return vmem_call(third_kernel, out_shape, where, own, *arrived, *expands)


def middle_kernel(
    where_ref, own_ref, arrived_ref, gate_expand_ref, up_expand_ref, down_reduce_ref,
    send_ref, keep_ref, gate_out, up_out, down_out, expands_ref, grads_ref,
):
    core, z = where_ref[0], where_ref[2]
    rank, piece = gate_expand_ref.shape
    rows = own_ref.shape[0]
    sums = own_ref[...] + arrived_ref[:rows].astype(F32)
    for kind, ref in enumerate((gate_expand_ref, up_expand_ref, down_reduce_ref)):
        expands_ref[z, kind] = ref[...]
        expands_ref[1 - z, kind] = arrived_ref[rows + kind * rank : rows + (kind + 1) * rank, :piece]
    lows = [sums[6 * piece + k * rank : 6 * piece + (k + 1) * rank].astype(BF16) for k in range(3)]
    keeps, sends, ranks = [], [], [0.0] * 3
    first = core == 0
    for chip in range(2):
        start = 3 * piece * chip
        gate, upper, back = [
            sums[start + kind * piece : start + (kind + 1) * piece]
            + SCALE * dot(expands_ref[chip, kind], lows[kind], 0, 0)
            for kind in range(3)
        ]
        sigma = jax.nn.sigmoid(gate)
        activated = gate * sigma
        hidden = activated * upper
        grad_gate = back * upper * sigma * (1.0 + gate * (1.0 - sigma))
        grad_upper = back * activated
        keeps.append(jnp.where(first, grad_gate, grad_upper))
        sends.append(jnp.where(first, grad_upper, grad_gate))
        for kind, grad in enumerate((grad_gate, grad_upper, hidden)):
            grads_ref[chip, kind] = grad.astype(BF16)
            ranks[kind] = ranks[kind] + dot(expands_ref[chip, kind], grads_ref[chip, kind], 1, 0)
    keep_ref[...] = jnp.concatenate([*keeps, *ranks], axis=0)
    send_ref[...] = jnp.concatenate([*sends, *ranks], axis=0).astype(BF16)
    for kind, out_ref in enumerate((gate_out, up_out, down_out)):
        out_ref[...] = SCALE * dot(lows[kind], grads_ref[z, kind], 1, 1)


def middle(where, own, arrived, expands):
    rank, piece = expands[0].shape
    tokens = own.shape[1]
    rows = 2 * piece + 3 * rank
    out_shape = [
        jax.ShapeDtypeStruct((rows, tokens), BF16),
        jax.ShapeDtypeStruct((rows, tokens), F32),
    ] + [jax.ShapeDtypeStruct((rank, piece), F32)] * 3
    scratch = [pltpu.VMEM((2, 3, rank, piece), BF16), pltpu.VMEM((2, 3, piece, tokens), BF16)]
    return vmem_call(middle_kernel, out_shape, where, own, arrived, *expands, scratch=scratch)


def pair_kernel(piece, where_ref, keep_ref, arrived_ref, out_ref):
    first = where_ref[0] == 0
    kept, arrived = keep_ref[...], arrived_ref[...].astype(F32)
    rows = []
    for chip in range(2):
        here = slice(chip * piece, (chip + 1) * piece)
        rows.append(jnp.where(first, kept[here], arrived[here]))
        rows.append(jnp.where(first, arrived[here], kept[here]))
    rows.append(kept[2 * piece :] + arrived[2 * piece :])
    out_ref[...] = jnp.concatenate(rows, axis=0).astype(BF16)


def pair_block(where, keep, arrived, piece):
    rows, tokens = keep.shape
    out_shape = [jax.ShapeDtypeStruct((rows + 2 * piece, tokens), BF16)]
    return vmem_call(functools.partial(pair_kernel, piece), out_shape, where, keep, arrived)[0]


def join_kernel(slot, where_ref, own_ref, *refs):
    arrived, out_ref = refs[:-1], refs[-1]
    count = len(refs)
    unit = (out_ref.shape[0] - own_ref.shape[0]) // (count - 1)
    place = where_ref[slot]
    rank = own_ref[unit:].astype(F32)
    for offset, ref in enumerate([own_ref, *arrived]):
        start = pl.multiple_of(lax.rem(place + count - offset, count) * unit, 16)
        out_ref[pl.ds(start, unit), :] = ref[:unit]
        if offset:
            rank = rank + ref[unit:].astype(F32)
    out_ref[count * unit :] = rank.astype(BF16)


def join(slot, where, own, arrived, rank_rows):
    rows, tokens = own.shape
    out_shape = [jax.ShapeDtypeStruct((rows + len(arrived) * (rows - rank_rows), tokens), BF16)]
    return vmem_call(functools.partial(join_kernel, slot), out_shape, where, own, *arrived)[0]


def back_kernel(last, *refs):
    if last:
        (where_ref, *pieces, gate_ref, up_ref, before_ref, rank_ref,
         own_ref, to_one, to_two, to_three, grads_ref, total_ref, turned_ref) = refs
    else:
        where_ref, *pieces, gate_ref, up_ref, total_ref, rank_ref, grads_ref = refs
    core = 1 - where_ref[0] if last else where_ref[0]
    place = where_ref[4] if last else where_ref[3]
    part = grads_ref.shape[0] // 4
    unit = part // 8
    for offset, ref in enumerate(pieces):
        there = lax.rem(place + 4 - offset, 4)
        for other in range(4):
            for z in range(2):
                chip = chip_of(core, there, z, other)
                source = (other * 2 + z) * unit
                grads_ref[pl.ds(pl.multiple_of(chip * unit, 16), unit), :] = ref[source : source + unit]

    for turn, weight_ref in enumerate((gate_ref, up_ref)):

        @pl.when(core == turn)
        def _():
            product = dot(weight_ref[...], grads_ref[...], 1, 0)
            total_ref[...] = product + before_ref[...] if last else product

    if last:
        turned_ref[...] = total_ref[...].T
        share = turned_ref.shape[0] // 4
        for offset, out_ref in enumerate([own_ref, to_one, to_two, to_three]):
            start = pl.multiple_of(lax.rem(where_ref[1] + offset, 4) * share, share)
            piece = turned_ref[pl.ds(start, share), :]
            block = jnp.concatenate([piece[:, :BLOCK], piece[:, BLOCK:], rank_ref[...]], axis=0)
            out_ref[...] = block.astype(BF16)
    else:
        rank = pieces[0][part:].astype(F32)
        for ref in pieces[1:]:
            rank = rank + ref[part:].astype(F32)
        rank_ref[...] = rank


def back(last, where, pieces, gate_weight, up_weight, before=()):
    width, hidden = gate_weight.shape
    rows, tokens = pieces[0].shape
    rank_rows = rows - hidden // 4
    scratch = [pltpu.VMEM((hidden, tokens), BF16)]
    if last:
        out_shape = [jax.ShapeDtypeStruct((tokens // 4 * width // BLOCK + rank_rows, tokens), BF16)] * 4
        scratch += [pltpu.VMEM((width, tokens), F32), pltpu.VMEM((tokens, width), F32)]
    else:
        out_shape = [
            jax.ShapeDtypeStruct((width, tokens), F32),
            jax.ShapeDtypeStruct((rank_rows, tokens), F32),
        ]
    return vmem_call(
        functools.partial(back_kernel, last), out_shape, where, *pieces, gate_weight, up_weight, *before,
        scratch=scratch,
    )


def last_kernel(
    where_ref, own_ref, one_ref, two_ref, three_ref, tokens_ref, gradient_ref, gate_reduce_ref, up_reduce_ref,
    input_out, gate_out, up_out, down_out, parts_ref, wide_ref,
):
    column = where_ref[1]
    for offset, ref in enumerate([own_ref, one_ref, two_ref, three_ref]):
        parts_ref[lax.rem(column + 4 - offset, 4)] = ref[...].astype(F32)
    summed = parts_ref[0] + parts_ref[1] + parts_ref[2] + parts_ref[3]
    share = input_out.shape[0]
    rank = gate_out.shape[0]
    sums = [summed[2 * share + k * rank : 2 * share + (k + 1) * rank].astype(BF16) for k in range(3)]
    wide_ref[...] = dot(sums[0], gate_reduce_ref[...], 0, 0) + dot(sums[1], up_reduce_ref[...], 0, 0)
    start = pl.multiple_of(column * share, share)
    main = jnp.concatenate([summed[:share], summed[share : 2 * share]], axis=1)
    input_out[...] = (main + SCALE * wide_ref[pl.ds(start, share), :]).astype(BF16)
    gate_out[...] = SCALE * dot(sums[0], tokens_ref[...], 1, 0)
    up_out[...] = SCALE * dot(sums[1], tokens_ref[...], 1, 0)
    down_out[...] = SCALE * dot(sums[2], gradient_ref[...], 1, 0)


def finish(where, own, others, tokens, gradient, gate_reduce, up_reduce):
    rank, width = gate_reduce.shape
    count = tokens.shape[0]
    vmem = pl.BlockSpec(memory_space=pltpu.VMEM)
    return pl.pallas_call(
        last_kernel,
        in_specs=[smem()] + [vmem] * 8,
        out_specs=[vmem] * 4,
        out_shape=[jax.ShapeDtypeStruct((count // 4, width), BF16)]
        + [jax.ShapeDtypeStruct((rank, width), F32)] * 3,
        scratch_shapes=[pltpu.VMEM((4,) + own.shape, F32), pltpu.VMEM((count, width), F32)],
        compiler_params=params(),
    )(where, own, *others, tokens, gradient, gate_reduce, up_reduce)


def per_device(
    tokens,
    output_gradient,
    gate_values,
    gate_scales,
    up_values,
    up_scales,
    down_values,
    down_scales,
    gate_reduce_factor,
    gate_expand,
    up_reduce_factor,
    up_expand,
    down_reduce,
    down_expand,
):
    piece = gate_expand.shape[1]
    position = lax.axis_index("row")
    core, y, z, x = position & 1, (position >> 1) & 3, (position >> 3) & 1, position >> 4
    first, second_place = jnp.where(core == 0, x, y), jnp.where(core == 0, y, x)
    where = jnp.stack([core, lax.axis_index("col"), z, first, second_place]).astype(jnp.int32)

    def exchange(value):
        return lax.ppermute(value, "row", [(i, i ^ 1) for i in range(64)])

    def along_z(value):
        return lax.ppermute(value, "row", [(i, i ^ 8) for i in range(64)])

    def along(second_axis, values):
        out = [None] * 3
        for offset in (2, 1, 3):
            pairs = []
            for i in range(64):
                if (i % 2 == 0) != second_axis:
                    pairs.append((i, (i + 16 * offset) % 64))
                else:
                    pairs.append((i, i - (i // 2 % 4) * 2 + ((i // 2 + offset) % 4) * 2))
            out[offset - 1] = lax.ppermute(values[offset - 1], "row", pairs)
        return out

    expands = (gate_expand, up_expand, down_reduce)
    *wide, low = wide_sums(
        where, gate_scales, up_scales, tokens, output_gradient, gate_reduce_factor, up_reduce_factor, down_expand,
        gate_values, up_values, piece,
    )
    tall = tall_sums(where, down_scales.T, output_gradient, down_values, piece, low)
    sends = [wide[0], wide[2], tall[0], low]
    own, *out = pack(where, [wide[1], wide[3], tall[1], low], [exchange(send) for send in sends])
    gate_weight, up_weight = weights(gate_scales, up_scales, gate_values, up_values, own)
    own, *out = second(where, own, along(False, out), piece, (gate_weight, up_weight))
    own, out = third(where, own, along(True, out), expands)
    send, keep, gate_expand_gradient, up_expand_gradient, down_reduce_gradient = middle(
        where, own, along_z(out), expands
    )
    rank_rows = low.shape[0]
    block = pair_block(where, keep, exchange(send), piece)
    block = join(4, where, block, along(True, [block] * 3), rank_rows)
    mine = [block, *along(False, [block] * 3)]
    theirs = [exchange(value) for value in mine]
    begun = back(False, where, mine, gate_weight, up_weight)
    own, *out = back(True, where, theirs, gate_weight, up_weight, begun)
    others = [
        lax.ppermute(value, "col", [(i, (i + offset) % 4) for i in range(4)])
        for offset, value in zip((1, 2, 3), out)
    ]
    input_gradient, gate_reduce_gradient, up_reduce_gradient, down_expand_gradient = finish(
        where, own, others, tokens, output_gradient, gate_reduce_factor, up_reduce_factor
    )
    return (
        input_gradient,
        gate_reduce_gradient,
        gate_expand_gradient,
        up_reduce_gradient,
        up_expand_gradient,
        down_reduce_gradient,
        down_expand_gradient,
    )


def solution(mesh):
    in_specs = (
        P(None, "row"),
        P(None, "row"),
        P("row", "col"),
        P("row", "col"),
        P("row", "col"),
        P("row", "col"),
        P("col", "row"),
        P("col", "row"),
        P(None, "row"),
        P(None, ("col", "row")),
        P(None, "row"),
        P(None, ("col", "row")),
        P(None, ("col", "row")),
        P(None, "row"),
    )
    out_specs = (
        P("col", "row"),
        P(None, "row"),
        P(None, ("col", "row")),
        P(None, "row"),
        P(None, ("col", "row")),
        P(None, ("col", "row")),
        P(None, "row"),
    )
    return jax.shard_map(
        per_device, mesh=mesh, in_specs=in_specs, out_specs=out_specs, check_vma=False
    )
```

```python
import functools

import jax
import jax.numpy as jnp
from jax import lax
from jax.experimental import pallas as pl
from jax.experimental.pallas import tpu as pltpu
from jax.sharding import PartitionSpec as P

BLOCK = 128
SCALE = 0.5
STEPS = 4
BF16 = jnp.bfloat16
F32 = jnp.float32
LIMIT = 32 * 1024 * 1024
CHUNK = 512
FIRST_PARTS = (1024, 2048, 3584)
LATER_PARTS = (6656,)
PIECES = (0, 1, 3, 2)


def params():
    return pltpu.CompilerParams(vmem_limit_bytes=LIMIT)


def dot(left, right, left_dim, right_dim):
    return lax.dot_general(
        left, right, (((left_dim,), (right_dim,)), ((), ())), preferred_element_type=F32
    )


def whole(shape):
    return pl.BlockSpec(shape, lambda *_: (0,) * len(shape))


def smem():
    return pl.BlockSpec(memory_space=pltpu.SMEM)


def dequantize_wide(values, scales_ref, first):
    columns = []
    for block in range(values.shape[1] // BLOCK):
        columns.append(
            jnp.concatenate(
                [
                    (values[part * BLOCK : (part + 1) * BLOCK, block * BLOCK : (block + 1) * BLOCK].astype(F32)
                     * scales_ref[part, first + block]).astype(BF16)
                    for part in range(values.shape[0] // BLOCK)
                ],
                axis=0,
            )
        )
    return jnp.concatenate(columns, axis=1)


def dequantize_tall(values, scales_ref, first):
    rows = []
    for block in range(values.shape[0] // BLOCK):
        rows.append(
            jnp.concatenate(
                [
                    (values[block * BLOCK : (block + 1) * BLOCK, part * BLOCK : (part + 1) * BLOCK].astype(F32)
                     * scales_ref[part, first + block]).astype(BF16)
                    for part in range(values.shape[1] // BLOCK)
                ],
                axis=1,
            )
        )
    return jnp.concatenate(rows, axis=0)


def split_by_core(core, sums_ref, send_ref, keep_ref):
    piece = send_ref.shape[1]
    for chip in range(sums_ref.shape[0] // (2 * piece)):
        start = chip * 2 * piece
        mine = pl.multiple_of(start + core * piece, 8)
        theirs = pl.multiple_of(start + (1 - core) * piece, 8)
        keep_ref[chip] = sums_ref[pl.ds(mine, piece), :].astype(BF16)
        send_ref[chip] = sums_ref[pl.ds(theirs, piece), :].astype(BF16)


def stay(value):
    return pltpu.with_memory_space_constraint(value, pltpu.HBM)


def fetch_all(sources, buffers, sems):
    copies = [pltpu.make_async_copy(s, b, sems.at[i]) for i, (s, b) in enumerate(zip(sources, buffers))]
    for copy in copies:
        copy.start()
    return copies


def start_parts(values_ref, buffer_ref, sems, axis, sizes):
    parts, first = [], 0
    for step, size in enumerate(sizes):
        part = pl.ds(first, size)
        place = (part, slice(None)) if axis == 0 else (slice(None), part)
        copy = pltpu.make_async_copy(values_ref.at[place], buffer_ref.at[place], sems.at[step])
        copy.start()
        parts.append((copy, first, size))
        first += size
    return parts


def wide_kernel(
    where_ref, gate_scales_hbm, up_scales_hbm, tokens_hbm, gradient_hbm, gate_reduce_hbm, up_reduce_hbm,
    down_expand_hbm, gate_hbm, up_hbm, gate_send, gate_keep, up_send, up_keep,
    gate_scales, up_scales, tokens_ref, gradient_ref, gate_reduce_ref, up_reduce_ref, down_expand_ref, gate_ref, up_ref, sums_ref, small, sems,
):
    small_copies = fetch_all(
        [gate_scales_hbm, tokens_hbm, up_scales_hbm, gradient_hbm, gate_reduce_hbm, up_reduce_hbm, down_expand_hbm],
        [gate_scales, tokens_ref, up_scales, gradient_ref, gate_reduce_ref, up_reduce_ref, down_expand_ref],
        small,
    )
    gate_parts = start_parts(gate_hbm, gate_ref, sems.at[0], 1, FIRST_PARTS)
    up_parts = start_parts(up_hbm, up_ref, sems.at[1], 1, LATER_PARTS)
    for copy in small_copies[:3]:
        copy.wait()
    for parts, values_ref, scales_ref, send_ref, keep_ref in (
        (gate_parts, gate_ref, gate_scales, gate_send, gate_keep),
        (up_parts, up_ref, up_scales, up_send, up_keep),
    ):
        for copy, first, size in parts:
            copy.wait()
            for start in range(first, first + size, CHUNK):
                part = slice(start, start + CHUNK)
                weight = dequantize_wide(values_ref[:, part], scales_ref, start // BLOCK)
                sums_ref[part] = dot(tokens_ref[...], weight, 1, 0).T
        split_by_core(where_ref[0], sums_ref, send_ref, keep_ref)
    for copy in small_copies[3:]:
        copy.wait()
    rank = gate_reduce_ref.shape[0]
    chips, rows = gate_keep.shape[0], 3 * rank // 2
    low = jnp.concatenate(
        [
            dot(gate_reduce_ref[...], tokens_ref[...], 1, 1),
            dot(up_reduce_ref[...], tokens_ref[...], 1, 1),
            dot(down_expand_ref[...], gradient_ref[...], 1, 1),
        ],
        axis=0,
    ).astype(BF16)
    for out_ref in (up_send, up_keep):
        for block in range(2):
            out_ref[chips + block, :rows] = low[block * rows : (block + 1) * rows]
            out_ref[chips + block, rows:] = jnp.zeros_like(out_ref[chips + block, rows:])


def tall_kernel(
    where_ref, scales_hbm, gradient_hbm, values_hbm, after_ref, send_ref, keep_ref,
    scales_ref, gradient_ref, values_ref, sums_ref, small, sems,
):
    small_copies = fetch_all([scales_hbm, gradient_hbm], [scales_ref, gradient_ref], small)
    parts = start_parts(values_hbm, values_ref, sems, 0, FIRST_PARTS)
    for copy in small_copies:
        copy.wait()
    for copy, first, size in parts:
        copy.wait()
        for start in range(first, first + size, CHUNK):
            part = slice(start, start + CHUNK)
            weight = dequantize_tall(values_ref[part], scales_ref, start // BLOCK)
            sums_ref[part] = dot(weight, gradient_ref[...], 1, 1)
    split_by_core(where_ref[0], sums_ref, send_ref, keep_ref)


def wide_sums(where, gate_scales, up_scales, tokens, gradient, gate_reduce, up_reduce, down_expand, gate, up, piece):
    width, hidden = gate.shape
    chips, count = hidden // (2 * piece), tokens.shape[0]
    vmem, hbm = pl.BlockSpec(memory_space=pltpu.VMEM), pl.BlockSpec(memory_space=pltpu.HBM)
    fetched = (tokens, gradient, gate_reduce, up_reduce, down_expand, gate, up)
    return pl.pallas_call(
        wide_kernel,
        in_specs=[smem()] + [hbm] * 9,
        out_specs=[vmem] * 4,
        out_shape=[jax.ShapeDtypeStruct((chips, piece, count), BF16)] * 2
        + [jax.ShapeDtypeStruct((chips + 2, piece, count), BF16)] * 2,
        scratch_shapes=[pltpu.SMEM(gate_scales.shape, F32)] * 2
        + [pltpu.VMEM(value.shape, BF16) for value in fetched]
        + [
            pltpu.VMEM((hidden, count), F32),
            pltpu.SemaphoreType.DMA((7,)),
            pltpu.SemaphoreType.DMA((2, len(FIRST_PARTS))),
        ],
        compiler_params=params(),
    )(where, *[stay(value) for value in (gate_scales, up_scales, *fetched)])


def tall_sums(where, scales, gradient, values, piece, after):
    hidden, width = values.shape
    chips, count = hidden // (2 * piece), gradient.shape[0]
    vmem, hbm = pl.BlockSpec(memory_space=pltpu.VMEM), pl.BlockSpec(memory_space=pltpu.HBM)
    return pl.pallas_call(
        tall_kernel,
        in_specs=[smem(), hbm, hbm, hbm, pl.BlockSpec(memory_space=pl.ANY)],
        out_specs=[vmem] * 2,
        out_shape=[jax.ShapeDtypeStruct((chips, piece, count), BF16)] * 2,
        scratch_shapes=[
            pltpu.SMEM(scales.shape, F32),
            pltpu.VMEM(gradient.shape, BF16),
            pltpu.VMEM(values.shape, BF16),
            pltpu.VMEM((hidden, count), F32),
            pltpu.SemaphoreType.DMA((2,)),
            pltpu.SemaphoreType.DMA((len(FIRST_PARTS),)),
        ],
        compiler_params=params(),
    )(where, stay(scales), stay(gradient), stay(values), after)


def weights_kernel(
    gate_scales, up_scales, gate_ref, up_ref, gate_expand, up_expand, down_reduce, after_ref, gate_out, up_out, expand_ref
):
    @pl.when(pl.program_id(0) == 0)
    def _():
        for kind, ref in enumerate((gate_expand, up_expand, down_reduce)):
            expand_ref[kind] = ref[...]

    first = pl.program_id(0) * (gate_ref.shape[1] // BLOCK)
    gate_out[...] = dequantize_wide(gate_ref[...], gate_scales, first)
    up_out[...] = dequantize_wide(up_ref[...], up_scales, first)


def weights(gate_scales, up_scales, gate, up, expands, after):
    width, hidden = gate.shape
    small = expands[0].shape
    block = pl.BlockSpec((width, hidden // STEPS), lambda i: (0, i))
    return pl.pallas_call(
        weights_kernel,
        grid=(STEPS,),
        in_specs=[smem(), smem(), block, block] + [whole(small)] * 3 + [pl.BlockSpec(memory_space=pl.ANY)],
        out_specs=[block] * 2 + [whole((3,) + small)],
        out_shape=[jax.ShapeDtypeStruct(gate.shape, BF16)] * 2 + [jax.ShapeDtypeStruct((3,) + small, BF16)],
        compiler_params=params(),
        cost_estimate=pl.CostEstimate(
            flops=2 * width * hidden, bytes_accessed=8 * width * hidden, transcendentals=0
        ),
    )(gate_scales, up_scales, gate, up, *expands, after)


def vmem_call(kernel, out_shape, *args, scratch=(), unread=0):
    vmem = pl.BlockSpec(memory_space=pltpu.VMEM)
    return pl.pallas_call(
        kernel,
        in_specs=[smem()] + [vmem] * (len(args) - 1 - unread) + [pl.BlockSpec(memory_space=pl.ANY)] * unread,
        out_specs=[vmem] * len(out_shape),
        out_shape=out_shape,
        scratch_shapes=scratch,
        compiler_params=params(),
    )(*args)


def chip_of(core, first, z, second):
    return jnp.where(core == 0, first * 8 + z * 4 + second, second * 8 + z * 4 + first)


def pack_rows(where_ref, keeps, received, offset, step):
    there = lax.rem(where_ref[3] + offset, 4)
    parts = []
    for near in range(2):
        chip = chip_of(where_ref[0], there, near, lax.rem(where_ref[4] + step, 4))
        parts += [keep[chip].astype(F32) + got[chip].astype(F32) for keep, got in zip(keeps, received)]
    return jnp.concatenate(parts, axis=0)


def pack_low(keep_ref, received_ref, rows):
    blocks = keep_ref.shape[0] - 2
    return jnp.concatenate(
        [keep_ref[blocks + i, :rows].astype(F32) + received_ref[blocks + i, :rows].astype(F32) for i in range(2)],
        axis=0,
    )


def stage_kernel(kinds, offsets, where_ref, *refs):
    keeps, received, outs = refs[:kinds], refs[kinds : 2 * kinds], refs[-len(offsets) :]
    pair = 2 * kinds * keeps[0].shape[1]
    for offset, out_ref in zip(offsets, outs):
        for step in range(4):
            rows = pack_rows(where_ref, keeps, received, offset, step)
            out_ref[step * pair : (step + 1) * pair] = rows.astype(out_ref.dtype)
        low_rows = out_ref.shape[0] - 4 * pair
        if low_rows:
            out_ref[4 * pair :] = pack_low(keeps[-1], received[-1], low_rows // 2).astype(out_ref.dtype)


def stage(offsets, where, keeps, received, low_rows=0, after=()):
    chips, piece, tokens = keeps[0].shape
    rows = 8 * len(keeps) * piece + low_rows
    out_shape = [jax.ShapeDtypeStruct((rows, tokens), BF16 if offset else F32) for offset in offsets]
    kernel = functools.partial(stage_kernel, len(keeps), offsets)
    return vmem_call(kernel, out_shape, where, *keeps, *received, *after, unread=len(after))


def second_kernel(where_ref, *refs):
    wide, tall, outs = refs[:4], refs[4:8], refs[-4:]
    down = tall[0].shape[0] // 4
    pair = 2 * down

    def add(refs, first, count):
        rows = slice(first, first + count)
        total = refs[0][rows]
        for ref in refs[1:]:
            total = total + ref[rows].astype(F32)
        return total

    low = add(wide, 4 * pair, wide[0].shape[0] - 4 * pair)
    for step, out_ref in enumerate(outs):
        out_ref[:pair] = add(wide, step * pair, pair).astype(out_ref.dtype)
        out_ref[pair : pair + down] = add(tall, step * down, down).astype(out_ref.dtype)
        out_ref[pair + down :] = low.astype(out_ref.dtype)


def second(where, wide, tall, piece, ready):
    rows, tokens = wide[0].shape
    rows -= 10 * piece
    out_shape = [jax.ShapeDtypeStruct((rows, tokens), F32 if i == 0 else BF16) for i in range(4)]
    return vmem_call(second_kernel, out_shape, where, *wide, *tall, *ready, unread=len(ready))


def third_kernel(where_ref, own_ref, one_ref, two_ref, three_ref, expand_ref, keep_ref, send_ref):
    rows, count = keep_ref.shape
    arrived = one_ref[...].astype(F32) + two_ref[...].astype(F32) + three_ref[...].astype(F32)
    everything = own_ref[...] + arrived
    keep_ref[...] = everything
    send_ref[:rows] = everything.astype(BF16)
    _, rank, piece = expand_ref.shape
    for kind in range(3):
        place = slice(rows + kind * rank, rows + (kind + 1) * rank)
        send_ref[place, :piece] = expand_ref[kind]
        send_ref[place, piece:] = jnp.zeros((rank, count - piece), BF16)


def third(where, own, arrived, expand):
    rows, count = own.shape
    far_rows = rows + 3 * expand.shape[1]
    out_shape = [jax.ShapeDtypeStruct(own.shape, F32), jax.ShapeDtypeStruct((far_rows, count), BF16)]
    return vmem_call(third_kernel, out_shape, where, own, *arrived, expand)


def middle_kernel(
    where_ref, own_ref, arrived_ref, expand_ref,
    send_ref, keep_ref, gate_out, up_out, down_out, expands_ref, grads_ref, ranks_ref,
):
    core, z = where_ref[0], where_ref[2]
    _, rank, piece = expand_ref.shape
    half = rank // 2
    rows = own_ref.shape[0]
    sums = own_ref[...] + arrived_ref[:rows].astype(F32)
    expands_ref[z] = expand_ref[...]
    for kind in range(3):
        expands_ref[1 - z, kind] = arrived_ref[rows + kind * rank : rows + (kind + 1) * rank, :piece]
    lows = [sums[6 * piece + k * rank : 6 * piece + (k + 1) * rank].astype(BF16) for k in range(3)]
    keeps, sends, ranks = [], [], [0.0] * 3
    for chip in range(2):
        starts = (2 * piece * chip, 2 * piece * chip + piece, 4 * piece + piece * chip)
        gate, upper, back = [
            sums[start : start + piece] + SCALE * dot(expands_ref[chip, kind], lows[kind], 0, 0)
            for kind, start in enumerate(starts)
        ]
        sigma = jax.nn.sigmoid(gate)
        activated = gate * sigma
        hidden = activated * upper
        grad_gate = back * upper * sigma * (1.0 + gate * (1.0 - sigma))
        grad_upper = back * activated
        keeps.append(jnp.where(core == 0, grad_gate, grad_upper))
        sends.append(jnp.where(core == 0, grad_upper, grad_gate))
        for kind, grad in enumerate((grad_gate, grad_upper, hidden)):
            grads_ref[chip, kind] = grad.astype(BF16)
            ranks[kind] = ranks[kind] + dot(expands_ref[chip, kind], grads_ref[chip, kind], 1, 0)
    for kind in range(3):
        ranks_ref[kind] = ranks[kind]
    mine = pl.multiple_of(core * half, half)
    theirs = pl.multiple_of((1 - core) * half, half)
    keeps += [ranks_ref[kind, pl.ds(mine, half), :] for kind in range(3)]
    sends += [ranks_ref[kind, pl.ds(theirs, half), :] for kind in range(3)]
    keep_ref[...] = jnp.concatenate(keeps, axis=0)
    send_ref[...] = jnp.concatenate(sends, axis=0).astype(BF16)
    for kind, out_ref in enumerate((gate_out, up_out, down_out)):
        out_ref[...] = SCALE * dot(lows[kind], grads_ref[z, kind], 1, 1)


def middle(where, own, arrived, expand):
    _, rank, piece = expand.shape
    tokens = own.shape[1]
    rows = 2 * piece + 3 * rank // 2
    out_shape = [
        jax.ShapeDtypeStruct((rows, tokens), BF16),
        jax.ShapeDtypeStruct((rows, tokens), F32),
    ] + [jax.ShapeDtypeStruct((rank, piece), F32)] * 3
    scratch = [
        pltpu.VMEM((2, 3, rank, piece), BF16),
        pltpu.VMEM((2, 3, piece, tokens), BF16),
        pltpu.VMEM((3, rank, tokens), F32),
    ]
    return vmem_call(middle_kernel, out_shape, where, own, arrived, expand, scratch=scratch)


def pair_kernel(piece, where_ref, keep_ref, arrived_ref, out_ref):
    first = where_ref[0] == 0
    kept, arrived = keep_ref[...], arrived_ref[...].astype(F32)
    rows = []
    for chip in range(2):
        here = slice(chip * piece, (chip + 1) * piece)
        rows.append(jnp.where(first, kept[here], arrived[here]))
        rows.append(jnp.where(first, arrived[here], kept[here]))
    rows.append(kept[2 * piece :] + arrived[2 * piece :])
    out_ref[...] = jnp.concatenate(rows, axis=0).astype(BF16)


def pair_block(where, keep, arrived, piece):
    rows, tokens = keep.shape
    out_shape = [jax.ShapeDtypeStruct((rows + 2 * piece, tokens), BF16)]
    return vmem_call(functools.partial(pair_kernel, piece), out_shape, where, keep, arrived)[0]


def join_kernel(slot, where_ref, own_ref, *refs):
    arrived, out_ref = refs[:-1], refs[-1]
    count = len(refs)
    unit = (out_ref.shape[0] - own_ref.shape[0]) // (count - 1)
    place = where_ref[slot]
    rank = own_ref[unit:].astype(F32)
    for offset, ref in zip(PIECES, [own_ref, *arrived]):
        start = pl.multiple_of(lax.rem(place + count - offset, count) * unit, 16)
        out_ref[pl.ds(start, unit), :] = ref[:unit]
        if offset:
            rank = rank + ref[unit:].astype(F32)
    out_ref[count * unit :] = rank.astype(BF16)


def join(slot, where, own, arrived, rank_rows):
    rows, tokens = own.shape
    out_shape = [jax.ShapeDtypeStruct((rows + len(arrived) * (rows - rank_rows), tokens), BF16)]
    return vmem_call(functools.partial(join_kernel, slot), out_shape, where, own, *arrived)[0]


def back_kernel(last, *refs):
    if last:
        (where_ref, *pieces, gate_ref, up_ref, before_ref, rank_ref,
         own_ref, to_one, to_two, to_three, grads_ref, total_ref, turned_ref) = refs
    else:
        where_ref, *pieces, gate_ref, up_ref, total_ref, rank_ref, grads_ref = refs
    core = 1 - where_ref[0] if last else where_ref[0]
    place = where_ref[4] if last else where_ref[3]
    part = grads_ref.shape[0] // 4
    unit = part // 8
    for offset, ref in zip(PIECES, pieces):
        there = lax.rem(place + 4 - offset, 4)
        for other in range(4):
            for z in range(2):
                chip = chip_of(core, there, z, other)
                source = (other * 2 + z) * unit
                grads_ref[pl.ds(pl.multiple_of(chip * unit, 16), unit), :] = ref[source : source + unit]

    for turn, weight_ref in enumerate((gate_ref, up_ref)):

        @pl.when(core == turn)
        def _():
            product = dot(weight_ref[...], grads_ref[...], 1, 0)
            total_ref[...] = product + before_ref[...] if last else product

    rank = pieces[0][part:].astype(F32)
    for ref in pieces[1:]:
        rank = rank + ref[part:].astype(F32)
    if last:
        half = rank.shape[0] // 3
        ranks = []
        for kind in range(3):
            rows = slice(kind * half, (kind + 1) * half)
            ranks.append(jnp.where(core == 0, rank[rows], rank_ref[rows]))
            ranks.append(jnp.where(core == 0, rank_ref[rows], rank[rows]))
        turned_ref[...] = total_ref[...].T
        share = turned_ref.shape[0] // 4
        for offset, out_ref in enumerate([own_ref, to_one, to_two, to_three]):
            start = pl.multiple_of(lax.rem(where_ref[1] + offset, 4) * share, share)
            piece = turned_ref[pl.ds(start, share), :]
            block = jnp.concatenate([piece[:, :BLOCK], piece[:, BLOCK:], *ranks], axis=0)
            out_ref[...] = block.astype(BF16)
    else:
        rank_ref[...] = rank


def back(last, where, pieces, gate_weight, up_weight, before=()):
    width, hidden = gate_weight.shape
    rows, tokens = pieces[0].shape
    rank_rows = rows - hidden // 4
    scratch = [pltpu.VMEM((hidden, tokens), BF16)]
    if last:
        out_shape = [jax.ShapeDtypeStruct((tokens // 4 * width // BLOCK + 2 * rank_rows, tokens), BF16)] * 4
        scratch += [pltpu.VMEM((width, tokens), F32), pltpu.VMEM((tokens, width), F32)]
    else:
        out_shape = [
            jax.ShapeDtypeStruct((width, tokens), F32),
            jax.ShapeDtypeStruct((rank_rows, tokens), F32),
        ]
    return vmem_call(
        functools.partial(back_kernel, last), out_shape, where, *pieces, gate_weight, up_weight, *before,
        scratch=scratch,
    )


def last_kernel(
    where_ref, own_ref, one_ref, two_ref, three_ref, tokens_ref, gradient_ref, gate_reduce_ref, up_reduce_ref,
    input_out, gate_out, up_out, down_out, parts_ref, wide_ref,
):
    column = where_ref[1]
    for offset, ref in enumerate([own_ref, one_ref, two_ref, three_ref]):
        parts_ref[lax.rem(column + 4 - offset, 4)] = ref[...].astype(F32)
    summed = parts_ref[0] + parts_ref[1] + parts_ref[2] + parts_ref[3]
    share = input_out.shape[0]
    rank = gate_out.shape[0]
    sums = [summed[2 * share + k * rank : 2 * share + (k + 1) * rank].astype(BF16) for k in range(3)]
    wide_ref[...] = dot(sums[0], gate_reduce_ref[...], 0, 0) + dot(sums[1], up_reduce_ref[...], 0, 0)
    start = pl.multiple_of(column * share, share)
    main = jnp.concatenate([summed[:share], summed[share : 2 * share]], axis=1)
    input_out[...] = (main + SCALE * wide_ref[pl.ds(start, share), :]).astype(BF16)
    gate_out[...] = SCALE * dot(sums[0], tokens_ref[...], 1, 0)
    up_out[...] = SCALE * dot(sums[1], tokens_ref[...], 1, 0)
    down_out[...] = SCALE * dot(sums[2], gradient_ref[...], 1, 0)


def finish(where, own, others, tokens, gradient, gate_reduce, up_reduce):
    rank, width = gate_reduce.shape
    count = tokens.shape[0]
    vmem = pl.BlockSpec(memory_space=pltpu.VMEM)
    return pl.pallas_call(
        last_kernel,
        in_specs=[smem()] + [vmem] * 8,
        out_specs=[vmem] * 4,
        out_shape=[jax.ShapeDtypeStruct((count // 4, width), BF16)]
        + [jax.ShapeDtypeStruct((rank, width), F32)] * 3,
        scratch_shapes=[pltpu.VMEM((4,) + own.shape, F32), pltpu.VMEM((count, width), F32)],
        compiler_params=params(),
    )(where, own, *others, tokens, gradient, gate_reduce, up_reduce)


def per_device(
    tokens,
    output_gradient,
    gate_values,
    gate_scales,
    up_values,
    up_scales,
    down_values,
    down_scales,
    gate_reduce_factor,
    gate_expand,
    up_reduce_factor,
    up_expand,
    down_reduce,
    down_expand,
):
    piece = gate_expand.shape[1]
    position = lax.axis_index("row")
    core, y, z, x = position & 1, (position >> 1) & 3, (position >> 3) & 1, position >> 4
    first, second_place = jnp.where(core == 0, x, y), jnp.where(core == 0, y, x)
    where = jnp.stack([core, lax.axis_index("col"), z, first, second_place]).astype(jnp.int32)

    def exchange(value):
        return lax.ppermute(value, "row", [(i, i ^ 1) for i in range(64)])

    def along_z(value):
        return lax.ppermute(value, "row", [(i, i ^ 8) for i in range(64)])

    def along(second_axis, offset, value):
        pairs = []
        for i in range(64):
            if (i % 2 == 0) != second_axis:
                pairs.append((i, (i + 16 * offset) % 64))
            else:
                pairs.append((i, i - (i // 2 % 4) * 2 + ((i // 2 + offset) % 4) * 2))
        return lax.ppermute(value, "row", pairs)

    def along_all(second_axis, values, order=(2, 1, 3)):
        return [along(second_axis, offset, values[offset - 1]) for offset in order]

    low_rows = 3 * gate_expand.shape[0]
    gate_send, gate_keep, up_send, up_keep = wide_sums(
        where, gate_scales, up_scales, tokens, output_gradient, gate_reduce_factor, up_reduce_factor, down_expand,
        gate_values, up_values, piece,
    )
    down_send, down_keep = tall_sums(where, down_scales.T, output_gradient, down_values, piece, gate_keep)
    keeps, received = [gate_keep, up_keep], [exchange(gate_send), exchange(up_send)]
    own, *out = stage((0, 1, 2, 3), where, keeps, received, low_rows)
    wide = [own, *along_all(False, out, (1, 2, 3))]
    keeps, received = [down_keep], [exchange(down_send)]
    own, one, two = stage((0, 1, 2), where, keeps, received, after=(own,))
    (three,) = stage((3,), where, keeps, received, after=(wide[1],))
    tall = [own, along(False, 1, one), along(False, 2, two), along(False, 3, three)]
    gate_weight, up_weight, expand = weights(
        gate_scales, up_scales, gate_values, up_values, (gate_expand, up_expand, down_reduce), own
    )
    own, *out = second(where, wide, tall, piece, (gate_weight, up_weight))
    own, out = third(where, own, along_all(True, out), expand)
    send, keep, gate_expand_gradient, up_expand_gradient, down_reduce_gradient = middle(
        where, own, along_z(out), expand
    )
    rank_rows = low_rows // 2
    block = pair_block(where, keep, exchange(send), piece)
    block = join(4, where, block, along_all(True, [block] * 3, PIECES[1:]), rank_rows)
    mine = [block, *along_all(False, [block] * 3, PIECES[1:])]
    theirs = [exchange(value) for value in mine]
    begun = back(False, where, mine, gate_weight, up_weight)
    own, *out = back(True, where, theirs, gate_weight, up_weight, begun)
    others = [
        lax.ppermute(value, "col", [(i, (i + offset) % 4) for i in range(4)])
        for offset, value in zip((1, 2, 3), out)
    ]
    input_gradient, gate_reduce_gradient, up_reduce_gradient, down_expand_gradient = finish(
        where, own, others, tokens, output_gradient, gate_reduce_factor, up_reduce_factor
    )
    return (
        input_gradient,
        gate_reduce_gradient,
        gate_expand_gradient,
        up_reduce_gradient,
        up_expand_gradient,
        down_reduce_gradient,
        down_expand_gradient,
    )


def solution(mesh):
    in_specs = (
        P(None, "row"),
        P(None, "row"),
        P("row", "col"),
        P("row", "col"),
        P("row", "col"),
        P("row", "col"),
        P("col", "row"),
        P("col", "row"),
        P(None, "row"),
        P(None, ("col", "row")),
        P(None, "row"),
        P(None, ("col", "row")),
        P(None, ("col", "row")),
        P(None, "row"),
    )
    out_specs = (
        P("col", "row"),
        P(None, "row"),
        P(None, ("col", "row")),
        P(None, "row"),
        P(None, ("col", "row")),
        P(None, ("col", "row")),
        P(None, "row"),
    )
    return jax.shard_map(
        per_device, mesh=mesh, in_specs=in_specs, out_specs=out_specs, check_vma=False
    )
```

```python
import functools

import jax
import jax.numpy as jnp
from jax import lax
from jax.experimental import pallas as pl
from jax.experimental.pallas import tpu as pltpu
from jax.sharding import PartitionSpec as P

BLOCK = 128
SCALE = 0.5
STEPS = 4
BF16 = jnp.bfloat16
F32 = jnp.float32
LIMIT = 32 * 1024 * 1024
CHUNK = 512
FIRST_PARTS = (1024, 2048, 3584)
LATER_PARTS = (6656,)
PIECES = (0, 1, 3, 2)


def params():
    return pltpu.CompilerParams(vmem_limit_bytes=LIMIT)


def dot(left, right, left_dim, right_dim):
    return lax.dot_general(
        left, right, (((left_dim,), (right_dim,)), ((), ())), preferred_element_type=F32
    )


def whole(shape):
    return pl.BlockSpec(shape, lambda *_: (0,) * len(shape))


def smem():
    return pl.BlockSpec(memory_space=pltpu.SMEM)


def dequantize_wide(values, scales_ref, first):
    columns = []
    for block in range(values.shape[1] // BLOCK):
        columns.append(
            jnp.concatenate(
                [
                    (values[part * BLOCK : (part + 1) * BLOCK, block * BLOCK : (block + 1) * BLOCK].astype(F32)
                     * scales_ref[part, first + block]).astype(BF16)
                    for part in range(values.shape[0] // BLOCK)
                ],
                axis=0,
            )
        )
    return jnp.concatenate(columns, axis=1)


def dequantize_tall(values, scales_ref, first):
    rows = []
    for block in range(values.shape[0] // BLOCK):
        rows.append(
            jnp.concatenate(
                [
                    (values[block * BLOCK : (block + 1) * BLOCK, part * BLOCK : (part + 1) * BLOCK].astype(F32)
                     * scales_ref[part, first + block]).astype(BF16)
                    for part in range(values.shape[1] // BLOCK)
                ],
                axis=1,
            )
        )
    return jnp.concatenate(rows, axis=0)


def split_by_core(core, sums_ref, send_ref, keep_ref):
    piece = send_ref.shape[1]
    for chip in range(sums_ref.shape[0] // (2 * piece)):
        start = chip * 2 * piece
        mine = pl.multiple_of(start + core * piece, 8)
        theirs = pl.multiple_of(start + (1 - core) * piece, 8)
        keep_ref[chip] = sums_ref[pl.ds(mine, piece), :].astype(BF16)
        send_ref[chip] = sums_ref[pl.ds(theirs, piece), :].astype(BF16)


def stay(value):
    return pltpu.with_memory_space_constraint(value, pltpu.HBM)


def fetch_all(sources, buffers, sems):
    copies = [pltpu.make_async_copy(s, b, sems.at[i]) for i, (s, b) in enumerate(zip(sources, buffers))]
    for copy in copies:
        copy.start()
    return copies


def start_parts(values_ref, buffer_ref, sems, axis, sizes):
    parts, first = [], 0
    for step, size in enumerate(sizes):
        part = pl.ds(first, size)
        place = (part, slice(None)) if axis == 0 else (slice(None), part)
        copy = pltpu.make_async_copy(values_ref.at[place], buffer_ref.at[place], sems.at[step])
        copy.start()
        parts.append((copy, first, size))
        first += size
    return parts


def wide_kernel(
    where_ref, gate_scales_hbm, up_scales_hbm, tokens_hbm, gradient_hbm, gate_reduce_hbm, up_reduce_hbm,
    down_expand_hbm, gate_hbm, up_hbm, gate_send, gate_keep, up_send, up_keep,
    gate_scales, up_scales, tokens_ref, gradient_ref, gate_reduce_ref, up_reduce_ref, down_expand_ref, gate_ref, up_ref, sums_ref, small, sems,
):
    small_copies = fetch_all(
        [gate_scales_hbm, tokens_hbm, up_scales_hbm, gradient_hbm, gate_reduce_hbm, up_reduce_hbm, down_expand_hbm],
        [gate_scales, tokens_ref, up_scales, gradient_ref, gate_reduce_ref, up_reduce_ref, down_expand_ref],
        small,
    )
    gate_parts = start_parts(gate_hbm, gate_ref, sems.at[0], 1, FIRST_PARTS)
    up_parts = start_parts(up_hbm, up_ref, sems.at[1], 1, LATER_PARTS)
    for copy in small_copies[:3]:
        copy.wait()
    for parts, values_ref, scales_ref, send_ref, keep_ref in (
        (gate_parts, gate_ref, gate_scales, gate_send, gate_keep),
        (up_parts, up_ref, up_scales, up_send, up_keep),
    ):
        for copy, first, size in parts:
            copy.wait()
            for start in range(first, first + size, CHUNK):
                part = slice(start, start + CHUNK)
                weight = dequantize_wide(values_ref[:, part], scales_ref, start // BLOCK)
                sums_ref[part] = dot(tokens_ref[...], weight, 1, 0).T
        split_by_core(where_ref[0], sums_ref, send_ref, keep_ref)
    for copy in small_copies[3:]:
        copy.wait()
    rank = gate_reduce_ref.shape[0]
    chips, rows = gate_keep.shape[0], 3 * rank // 2
    low = jnp.concatenate(
        [
            dot(gate_reduce_ref[...], tokens_ref[...], 1, 1),
            dot(up_reduce_ref[...], tokens_ref[...], 1, 1),
            dot(down_expand_ref[...], gradient_ref[...], 1, 1),
        ],
        axis=0,
    ).astype(BF16)
    for out_ref in (up_send, up_keep):
        for block in range(2):
            out_ref[chips + block, :rows] = low[block * rows : (block + 1) * rows]
            out_ref[chips + block, rows:] = jnp.zeros_like(out_ref[chips + block, rows:])


def tall_kernel(
    where_ref, scales_hbm, gradient_hbm, values_hbm, after_ref, send_ref, keep_ref,
    scales_ref, gradient_ref, values_ref, sums_ref, small, sems,
):
    small_copies = fetch_all([scales_hbm, gradient_hbm], [scales_ref, gradient_ref], small)
    parts = start_parts(values_hbm, values_ref, sems, 0, FIRST_PARTS)
    for copy in small_copies:
        copy.wait()
    for copy, first, size in parts:
        copy.wait()
        for start in range(first, first + size, CHUNK):
            part = slice(start, start + CHUNK)
            weight = dequantize_tall(values_ref[part], scales_ref, start // BLOCK)
            sums_ref[part] = dot(weight, gradient_ref[...], 1, 1)
    split_by_core(where_ref[0], sums_ref, send_ref, keep_ref)


def wide_sums(where, gate_scales, up_scales, tokens, gradient, gate_reduce, up_reduce, down_expand, gate, up, piece):
    width, hidden = gate.shape
    chips, count = hidden // (2 * piece), tokens.shape[0]
    vmem, hbm = pl.BlockSpec(memory_space=pltpu.VMEM), pl.BlockSpec(memory_space=pltpu.HBM)
    fetched = (tokens, gradient, gate_reduce, up_reduce, down_expand, gate, up)
    return pl.pallas_call(
        wide_kernel,
        in_specs=[smem()] + [hbm] * 9,
        out_specs=[vmem] * 4,
        out_shape=[jax.ShapeDtypeStruct((chips, piece, count), BF16)] * 2
        + [jax.ShapeDtypeStruct((chips + 2, piece, count), BF16)] * 2,
        scratch_shapes=[pltpu.SMEM(gate_scales.shape, F32)] * 2
        + [pltpu.VMEM(value.shape, BF16) for value in fetched]
        + [
            pltpu.VMEM((hidden, count), F32),
            pltpu.SemaphoreType.DMA((7,)),
            pltpu.SemaphoreType.DMA((2, len(FIRST_PARTS))),
        ],
        compiler_params=params(),
    )(where, *[stay(value) for value in (gate_scales, up_scales, *fetched)])


def tall_sums(where, scales, gradient, values, piece, after):
    hidden, width = values.shape
    chips, count = hidden // (2 * piece), gradient.shape[0]
    vmem, hbm = pl.BlockSpec(memory_space=pltpu.VMEM), pl.BlockSpec(memory_space=pltpu.HBM)
    return pl.pallas_call(
        tall_kernel,
        in_specs=[smem(), hbm, hbm, hbm, pl.BlockSpec(memory_space=pl.ANY)],
        out_specs=[vmem] * 2,
        out_shape=[jax.ShapeDtypeStruct((chips, piece, count), BF16)] * 2,
        scratch_shapes=[
            pltpu.SMEM(scales.shape, F32),
            pltpu.VMEM(gradient.shape, BF16),
            pltpu.VMEM(values.shape, BF16),
            pltpu.VMEM((hidden, count), F32),
            pltpu.SemaphoreType.DMA((2,)),
            pltpu.SemaphoreType.DMA((len(FIRST_PARTS),)),
        ],
        compiler_params=params(),
    )(where, stay(scales), stay(gradient), stay(values), after)


def weights_kernel(
    gate_scales, up_scales, gate_ref, up_ref, gate_expand, up_expand, down_reduce, after_ref, gate_out, up_out, expand_ref
):
    @pl.when(pl.program_id(0) == 0)
    def _():
        for kind, ref in enumerate((gate_expand, up_expand, down_reduce)):
            expand_ref[kind] = ref[...]

    first = pl.program_id(0) * (gate_ref.shape[1] // BLOCK)
    gate_out[...] = dequantize_wide(gate_ref[...], gate_scales, first)
    up_out[...] = dequantize_wide(up_ref[...], up_scales, first)


def weights(gate_scales, up_scales, gate, up, expands, after):
    width, hidden = gate.shape
    small = expands[0].shape
    block = pl.BlockSpec((width, hidden // STEPS), lambda i: (0, i))
    return pl.pallas_call(
        weights_kernel,
        grid=(STEPS,),
        in_specs=[smem(), smem(), block, block] + [whole(small)] * 3 + [pl.BlockSpec(memory_space=pl.ANY)],
        out_specs=[block] * 2 + [whole((3,) + small)],
        out_shape=[jax.ShapeDtypeStruct(gate.shape, BF16)] * 2 + [jax.ShapeDtypeStruct((3,) + small, BF16)],
        compiler_params=params(),
        cost_estimate=pl.CostEstimate(
            flops=2 * width * hidden, bytes_accessed=8 * width * hidden, transcendentals=0
        ),
    )(gate_scales, up_scales, gate, up, *expands, after)


def vmem_call(kernel, out_shape, *args, scratch=(), unread=0):
    vmem = pl.BlockSpec(memory_space=pltpu.VMEM)
    return pl.pallas_call(
        kernel,
        in_specs=[smem()] + [vmem] * (len(args) - 1 - unread) + [pl.BlockSpec(memory_space=pl.ANY)] * unread,
        out_specs=[vmem] * len(out_shape),
        out_shape=out_shape,
        scratch_shapes=scratch,
        compiler_params=params(),
    )(*args)


def chip_of(core, first, z, second):
    return jnp.where(core == 0, first * 8 + z * 4 + second, second * 8 + z * 4 + first)


def pack_rows(where_ref, keeps, received, offset, step):
    there = lax.rem(where_ref[3] + offset, 4)
    parts = []
    for near in range(2):
        chip = chip_of(where_ref[0], there, near, lax.rem(where_ref[4] + step, 4))
        parts += [keep[chip].astype(F32) + got[chip].astype(F32) for keep, got in zip(keeps, received)]
    return jnp.concatenate(parts, axis=0)


def pack_low(keep_ref, received_ref, rows):
    blocks = keep_ref.shape[0] - 2
    return jnp.concatenate(
        [keep_ref[blocks + i, :rows].astype(F32) + received_ref[blocks + i, :rows].astype(F32) for i in range(2)],
        axis=0,
    )


def stage_kernel(kinds, offsets, where_ref, *refs):
    keeps, received, outs = refs[:kinds], refs[kinds : 2 * kinds], refs[-len(offsets) :]
    pair = 2 * kinds * keeps[0].shape[1]
    for offset, out_ref in zip(offsets, outs):
        for step in range(4):
            rows = pack_rows(where_ref, keeps, received, offset, step)
            out_ref[step * pair : (step + 1) * pair] = rows.astype(out_ref.dtype)
        low_rows = out_ref.shape[0] - 4 * pair
        if low_rows:
            out_ref[4 * pair :] = pack_low(keeps[-1], received[-1], low_rows // 2).astype(out_ref.dtype)


def stage(offsets, where, keeps, received, low_rows=0, after=()):
    chips, piece, tokens = keeps[0].shape
    rows = 8 * len(keeps) * piece + low_rows
    out_shape = [jax.ShapeDtypeStruct((rows, tokens), BF16 if offset else F32) for offset in offsets]
    kernel = functools.partial(stage_kernel, len(keeps), offsets)
    return vmem_call(kernel, out_shape, where, *keeps, *received, *after, unread=len(after))


def second_kernel(where_ref, *refs):
    wide, tall, expand_ref, outs, expand_out = refs[:4], refs[4:8], refs[8], refs[-5:-1], refs[-1]
    expand_out[...] = expand_ref[...]
    down = tall[0].shape[0] // 4
    pair = 2 * down

    def add(refs, first, count):
        rows = slice(first, first + count)
        total = refs[0][rows]
        for ref in refs[1:]:
            total = total + ref[rows].astype(F32)
        return total

    low = add(wide, 4 * pair, wide[0].shape[0] - 4 * pair)
    for step, out_ref in enumerate(outs):
        out_ref[:pair] = add(wide, step * pair, pair).astype(out_ref.dtype)
        out_ref[pair : pair + down] = add(tall, step * down, down).astype(out_ref.dtype)
        out_ref[pair + down :] = low.astype(out_ref.dtype)


def second(where, wide, tall, expand, piece, ready):
    rows, tokens = wide[0].shape
    rows -= 10 * piece
    out_shape = [jax.ShapeDtypeStruct((rows, tokens), F32 if i == 0 else BF16) for i in range(4)]
    out_shape.append(jax.ShapeDtypeStruct(expand.shape, BF16))
    return vmem_call(second_kernel, out_shape, where, *wide, *tall, expand, *ready, unread=len(ready))


def third_kernel(where_ref, own_ref, one_ref, two_ref, three_ref, after_ref, keep_ref, send_ref):
    arrived = one_ref[...].astype(F32) + two_ref[...].astype(F32) + three_ref[...].astype(F32)
    everything = own_ref[...] + arrived
    keep_ref[...] = everything
    send_ref[...] = everything.astype(BF16)


def third(where, own, arrived, after):
    out_shape = [jax.ShapeDtypeStruct(own.shape, F32), jax.ShapeDtypeStruct(own.shape, BF16)]
    return vmem_call(third_kernel, out_shape, where, own, *arrived, after, unread=1)


def middle_kernel(
    where_ref, own_ref, arrived_ref, expand_ref, far_expand_ref,
    send_ref, keep_ref, gate_out, up_out, down_out, expands_ref, grads_ref, ranks_ref,
):
    core, z = where_ref[0], where_ref[2]
    _, rank, piece = expand_ref.shape
    half = rank // 2
    sums = own_ref[...] + arrived_ref[...].astype(F32)
    expands_ref[z] = expand_ref[...]
    expands_ref[1 - z] = far_expand_ref[...]
    lows = [sums[6 * piece + k * rank : 6 * piece + (k + 1) * rank].astype(BF16) for k in range(3)]
    keeps, sends, ranks = [], [], [0.0] * 3
    for chip in range(2):
        starts = (2 * piece * chip, 2 * piece * chip + piece, 4 * piece + piece * chip)
        gate, upper, back = [
            sums[start : start + piece] + SCALE * dot(expands_ref[chip, kind], lows[kind], 0, 0)
            for kind, start in enumerate(starts)
        ]
        sigma = jax.nn.sigmoid(gate)
        activated = gate * sigma
        hidden = activated * upper
        grad_gate = back * upper * sigma * (1.0 + gate * (1.0 - sigma))
        grad_upper = back * activated
        keeps.append(jnp.where(core == 0, grad_gate, grad_upper))
        sends.append(jnp.where(core == 0, grad_upper, grad_gate))
        for kind, grad in enumerate((grad_gate, grad_upper, hidden)):
            grads_ref[chip, kind] = grad.astype(BF16)
            ranks[kind] = ranks[kind] + dot(expands_ref[chip, kind], grads_ref[chip, kind], 1, 0)
    for kind in range(3):
        ranks_ref[kind] = ranks[kind]
    mine = pl.multiple_of(core * half, half)
    theirs = pl.multiple_of((1 - core) * half, half)
    keeps += [ranks_ref[kind, pl.ds(mine, half), :] for kind in range(3)]
    sends += [ranks_ref[kind, pl.ds(theirs, half), :] for kind in range(3)]
    keep_ref[...] = jnp.concatenate(keeps, axis=0)
    send_ref[...] = jnp.concatenate(sends, axis=0).astype(BF16)
    for kind, out_ref in enumerate((gate_out, up_out, down_out)):
        out_ref[...] = SCALE * dot(lows[kind], grads_ref[z, kind], 1, 1)


def middle(where, own, arrived, expand, far_expand):
    _, rank, piece = expand.shape
    tokens = own.shape[1]
    rows = 2 * piece + 3 * rank // 2
    out_shape = [
        jax.ShapeDtypeStruct((rows, tokens), BF16),
        jax.ShapeDtypeStruct((rows, tokens), F32),
    ] + [jax.ShapeDtypeStruct((rank, piece), F32)] * 3
    scratch = [
        pltpu.VMEM((2, 3, rank, piece), BF16),
        pltpu.VMEM((2, 3, piece, tokens), BF16),
        pltpu.VMEM((3, rank, tokens), F32),
    ]
    return vmem_call(middle_kernel, out_shape, where, own, arrived, expand, far_expand, scratch=scratch)


def pair_kernel(piece, where_ref, keep_ref, arrived_ref, out_ref):
    first = where_ref[0] == 0
    kept, arrived = keep_ref[...], arrived_ref[...].astype(F32)
    rows = []
    for chip in range(2):
        here = slice(chip * piece, (chip + 1) * piece)
        rows.append(jnp.where(first, kept[here], arrived[here]))
        rows.append(jnp.where(first, arrived[here], kept[here]))
    rows.append(kept[2 * piece :] + arrived[2 * piece :])
    out_ref[...] = jnp.concatenate(rows, axis=0).astype(BF16)


def pair_block(where, keep, arrived, piece):
    rows, tokens = keep.shape
    out_shape = [jax.ShapeDtypeStruct((rows + 2 * piece, tokens), BF16)]
    return vmem_call(functools.partial(pair_kernel, piece), out_shape, where, keep, arrived)[0]


def join_kernel(slot, where_ref, own_ref, *refs):
    arrived, out_ref = refs[:-1], refs[-1]
    count = len(refs)
    unit = (out_ref.shape[0] - own_ref.shape[0]) // (count - 1)
    place = where_ref[slot]
    rank = own_ref[unit:].astype(F32)
    for offset, ref in zip(PIECES, [own_ref, *arrived]):
        start = pl.multiple_of(lax.rem(place + count - offset, count) * unit, 16)
        out_ref[pl.ds(start, unit), :] = ref[:unit]
        if offset:
            rank = rank + ref[unit:].astype(F32)
    out_ref[count * unit :] = rank.astype(BF16)


def join(slot, where, own, arrived, rank_rows):
    rows, tokens = own.shape
    out_shape = [jax.ShapeDtypeStruct((rows + len(arrived) * (rows - rank_rows), tokens), BF16)]
    return vmem_call(functools.partial(join_kernel, slot), out_shape, where, own, *arrived)[0]


def back_kernel(last, *refs):
    if last:
        (where_ref, *pieces, gate_ref, up_ref, before_ref, rank_ref,
         keep_ref, send_ref, grads_ref, total_ref, turned_ref) = refs
    else:
        where_ref, *pieces, gate_ref, up_ref, total_ref, rank_ref, grads_ref = refs
    core = 1 - where_ref[0] if last else where_ref[0]
    place = where_ref[4] if last else where_ref[3]
    part = grads_ref.shape[0] // 4
    unit = part // 8
    for offset, ref in zip(PIECES, pieces):
        there = lax.rem(place + 4 - offset, 4)
        for other in range(4):
            for z in range(2):
                chip = chip_of(core, there, z, other)
                source = (other * 2 + z) * unit
                grads_ref[pl.ds(pl.multiple_of(chip * unit, 16), unit), :] = ref[source : source + unit]

    for turn, weight_ref in enumerate((gate_ref, up_ref)):

        @pl.when(core == turn)
        def _():
            product = dot(weight_ref[...], grads_ref[...], 1, 0)
            total_ref[...] = product + before_ref[...] if last else product

    rank = pieces[0][part:].astype(F32)
    for ref in pieces[1:]:
        rank = rank + ref[part:].astype(F32)
    if last:
        half = rank.shape[0] // 3
        ranks = []
        for kind in range(3):
            rows = slice(kind * half, (kind + 1) * half)
            ranks.append(jnp.where(core == 0, rank[rows], rank_ref[rows]))
            ranks.append(jnp.where(core == 0, rank_ref[rows], rank[rows]))
        turned_ref[...] = total_ref[...].T
        share = turned_ref.shape[0] // 4
        column = where_ref[1]
        for base, out_ref in ((column, keep_ref), (column ^ 1, send_ref)):
            rows = []
            for place in (base, 3 - base):
                piece = turned_ref[pl.ds(pl.multiple_of(place * share, share), share), :]
                rows += [piece[:, :BLOCK], piece[:, BLOCK:]]
            out_ref[...] = jnp.concatenate([*rows, *ranks], axis=0).astype(BF16)
    else:
        rank_ref[...] = rank


def back(last, where, pieces, gate_weight, up_weight, before=()):
    width, hidden = gate_weight.shape
    rows, tokens = pieces[0].shape
    rank_rows = rows - hidden // 4
    scratch = [pltpu.VMEM((hidden, tokens), BF16)]
    if last:
        out_shape = [jax.ShapeDtypeStruct((tokens // 2 * width // BLOCK + 2 * rank_rows, tokens), BF16)] * 2
        scratch += [pltpu.VMEM((width, tokens), F32), pltpu.VMEM((tokens, width), F32)]
    else:
        out_shape = [
            jax.ShapeDtypeStruct((width, tokens), F32),
            jax.ShapeDtypeStruct((rank_rows, tokens), F32),
        ]
    return vmem_call(
        functools.partial(back_kernel, last), out_shape, where, *pieces, gate_weight, up_weight, *before,
        scratch=scratch,
    )


def halfway_kernel(where_ref, own_ref, arrived_ref, main_ref, send_ref):
    rows = main_ref.shape[0]
    summed = own_ref[...].astype(F32) + arrived_ref[...].astype(F32)
    main_ref[...] = summed[:rows]
    send_ref[...] = summed[rows:].astype(BF16)


def halfway(where, own, arrived, main_rows):
    rows, tokens = own.shape
    out_shape = [
        jax.ShapeDtypeStruct((main_rows, tokens), F32),
        jax.ShapeDtypeStruct((rows - main_rows, tokens), BF16),
    ]
    return vmem_call(halfway_kernel, out_shape, where, own, arrived)


def last_kernel(
    where_ref, main_ref, own_ref, arrived_ref, tokens_ref, gradient_ref, gate_reduce_ref, up_reduce_ref,
    input_out, gate_out, up_out, down_out, wide_ref,
):
    share = input_out.shape[0]
    rank = gate_out.shape[0]
    main = main_ref[...] + arrived_ref[: 2 * share].astype(F32)
    summed = own_ref[2 * share :].astype(F32) + arrived_ref[2 * share :].astype(F32)
    sums = [summed[k * rank : (k + 1) * rank].astype(BF16) for k in range(3)]
    wide_ref[...] = dot(sums[0], gate_reduce_ref[...], 0, 0) + dot(sums[1], up_reduce_ref[...], 0, 0)
    start = pl.multiple_of(where_ref[1] * share, share)
    main = jnp.concatenate([main[:share], main[share:]], axis=1)
    input_out[...] = (main + SCALE * wide_ref[pl.ds(start, share), :]).astype(BF16)
    gate_out[...] = SCALE * dot(sums[0], tokens_ref[...], 1, 0)
    up_out[...] = SCALE * dot(sums[1], tokens_ref[...], 1, 0)
    down_out[...] = SCALE * dot(sums[2], gradient_ref[...], 1, 0)


def finish(where, main, own, arrived, tokens, gradient, gate_reduce, up_reduce):
    rank, width = gate_reduce.shape
    count = tokens.shape[0]
    out_shape = [jax.ShapeDtypeStruct((count // 4, width), BF16)] + [jax.ShapeDtypeStruct((rank, width), F32)] * 3
    return vmem_call(
        last_kernel, out_shape, where, main, own, arrived, tokens, gradient, gate_reduce, up_reduce,
        scratch=[pltpu.VMEM((count, width), F32)],
    )


def per_device(
    tokens,
    output_gradient,
    gate_values,
    gate_scales,
    up_values,
    up_scales,
    down_values,
    down_scales,
    gate_reduce_factor,
    gate_expand,
    up_reduce_factor,
    up_expand,
    down_reduce,
    down_expand,
):
    piece = gate_expand.shape[1]
    position = lax.axis_index("row")
    core, y, z, x = position & 1, (position >> 1) & 3, (position >> 3) & 1, position >> 4
    first, second_place = jnp.where(core == 0, x, y), jnp.where(core == 0, y, x)
    where = jnp.stack([core, lax.axis_index("col"), z, first, second_place]).astype(jnp.int32)

    def exchange(value):
        return lax.ppermute(value, "row", [(i, i ^ 1) for i in range(64)])

    def along_z(value):
        return lax.ppermute(value, "row", [(i, i ^ 8) for i in range(64)])

    def along(second_axis, offset, value):
        pairs = []
        for i in range(64):
            if (i % 2 == 0) != second_axis:
                pairs.append((i, (i + 16 * offset) % 64))
            else:
                pairs.append((i, i - (i // 2 % 4) * 2 + ((i // 2 + offset) % 4) * 2))
        return lax.ppermute(value, "row", pairs)

    def along_all(second_axis, values, order=(2, 1, 3)):
        return [along(second_axis, offset, values[offset - 1]) for offset in order]

    low_rows = 3 * gate_expand.shape[0]
    gate_send, gate_keep, up_send, up_keep = wide_sums(
        where, gate_scales, up_scales, tokens, output_gradient, gate_reduce_factor, up_reduce_factor, down_expand,
        gate_values, up_values, piece,
    )
    down_send, down_keep = tall_sums(where, down_scales.T, output_gradient, down_values, piece, gate_keep)
    keeps, received = [gate_keep, up_keep], [exchange(gate_send), exchange(up_send)]
    own, *out = stage((0, 1, 2, 3), where, keeps, received, low_rows)
    wide = [own, *along_all(False, out, (1, 2, 3))]
    keeps, received = [down_keep], [exchange(down_send)]
    own, one, two = stage((0, 1, 2), where, keeps, received, after=(own,))
    (three,) = stage((3,), where, keeps, received, after=(wide[1],))
    tall = [own, along(False, 1, one), along(False, 2, two), along(False, 3, three)]
    gate_weight, up_weight, expand = weights(
        gate_scales, up_scales, gate_values, up_values, (gate_expand, up_expand, down_reduce), own
    )
    own, *out, leaving = second(where, wide, tall, expand, piece, (gate_weight, up_weight))
    far_expand = along_z(leaving)
    own, out = third(where, own, along_all(True, out), far_expand)
    send, keep, gate_expand_gradient, up_expand_gradient, down_reduce_gradient = middle(
        where, own, along_z(out), expand, far_expand
    )
    rank_rows = low_rows // 2
    block = pair_block(where, keep, exchange(send), piece)
    block = join(4, where, block, along_all(True, [block] * 3, PIECES[1:]), rank_rows)
    mine = [block, *along_all(False, [block] * 3, PIECES[1:])]
    theirs = [exchange(value) for value in mine]
    begun = back(False, where, mine, gate_weight, up_weight)
    own, out = back(True, where, theirs, gate_weight, up_weight, begun)
    main, out = halfway(
        where, own, lax.ppermute(out, "col", [(i, i ^ 1) for i in range(4)]), tokens.size // 4 // BLOCK
    )
    arrived = lax.ppermute(out, "col", [(i, 3 - i) for i in range(4)])
    input_gradient, gate_reduce_gradient, up_reduce_gradient, down_expand_gradient = finish(
        where, main, out, arrived, tokens, output_gradient, gate_reduce_factor, up_reduce_factor
    )
    return (
        input_gradient,
        gate_reduce_gradient,
        gate_expand_gradient,
        up_reduce_gradient,
        up_expand_gradient,
        down_reduce_gradient,
        down_expand_gradient,
    )


def solution(mesh):
    in_specs = (
        P(None, "row"),
        P(None, "row"),
        P("row", "col"),
        P("row", "col"),
        P("row", "col"),
        P("row", "col"),
        P("col", "row"),
        P("col", "row"),
        P(None, "row"),
        P(None, ("col", "row")),
        P(None, "row"),
        P(None, ("col", "row")),
        P(None, ("col", "row")),
        P(None, "row"),
    )
    out_specs = (
        P("col", "row"),
        P(None, "row"),
        P(None, ("col", "row")),
        P(None, "row"),
        P(None, ("col", "row")),
        P(None, ("col", "row")),
        P(None, "row"),
    )
    return jax.shard_map(
        per_device, mesh=mesh, in_specs=in_specs, out_specs=out_specs, check_vma=False
    )
```

```python
import functools

import jax
import jax.numpy as jnp
from jax import lax
from jax.experimental import pallas as pl
from jax.experimental.pallas import tpu as pltpu
from jax.sharding import PartitionSpec as P

BLOCK = 128
SCALE = 0.5
STEPS = 4
BF16 = jnp.bfloat16
F32 = jnp.float32
LIMIT = 32 * 1024 * 1024
CHUNK = 512
FIRST_PARTS = (1024, 2048, 3584)
LATER_PARTS = (6656,)
PIECES = (0, 1, 3, 2)


def params():
    return pltpu.CompilerParams(vmem_limit_bytes=LIMIT)


def dot(left, right, left_dim, right_dim):
    return lax.dot_general(
        left, right, (((left_dim,), (right_dim,)), ((), ())), preferred_element_type=F32
    )


def whole(shape):
    return pl.BlockSpec(shape, lambda *_: (0,) * len(shape))


def smem():
    return pl.BlockSpec(memory_space=pltpu.SMEM)


def dequantize_wide(values, scales_ref, first):
    columns = []
    for block in range(values.shape[1] // BLOCK):
        columns.append(
            jnp.concatenate(
                [
                    (values[part * BLOCK : (part + 1) * BLOCK, block * BLOCK : (block + 1) * BLOCK].astype(F32)
                     * scales_ref[part, first + block]).astype(BF16)
                    for part in range(values.shape[0] // BLOCK)
                ],
                axis=0,
            )
        )
    return jnp.concatenate(columns, axis=1)


def dequantize_tall(values, scales_ref, first):
    rows = []
    for block in range(values.shape[0] // BLOCK):
        rows.append(
            jnp.concatenate(
                [
                    (values[block * BLOCK : (block + 1) * BLOCK, part * BLOCK : (part + 1) * BLOCK].astype(F32)
                     * scales_ref[part, first + block]).astype(BF16)
                    for part in range(values.shape[1] // BLOCK)
                ],
                axis=1,
            )
        )
    return jnp.concatenate(rows, axis=0)


def split_by_core(core, sums_ref, send_ref, keep_ref):
    piece = send_ref.shape[1]
    for chip in range(sums_ref.shape[0] // (2 * piece)):
        start = chip * 2 * piece
        mine = pl.multiple_of(start + core * piece, 8)
        theirs = pl.multiple_of(start + (1 - core) * piece, 8)
        keep_ref[chip] = sums_ref[pl.ds(mine, piece), :].astype(BF16)
        send_ref[chip] = sums_ref[pl.ds(theirs, piece), :].astype(BF16)


def stay(value):
    return pltpu.with_memory_space_constraint(value, pltpu.HBM)


def fetch_all(sources, buffers, sems):
    copies = [pltpu.make_async_copy(s, b, sems.at[i]) for i, (s, b) in enumerate(zip(sources, buffers))]
    for copy in copies:
        copy.start()
    return copies


def start_parts(values_ref, buffer_ref, sems, axis, sizes):
    parts, first = [], 0
    for step, size in enumerate(sizes):
        part = pl.ds(first, size)
        place = (part, slice(None)) if axis == 0 else (slice(None), part)
        copy = pltpu.make_async_copy(values_ref.at[place], buffer_ref.at[place], sems.at[step])
        copy.start()
        parts.append((copy, first, size))
        first += size
    return parts


def wide_kernel(
    where_ref, gate_scales_hbm, up_scales_hbm, tokens_hbm, gradient_hbm, gate_reduce_hbm, up_reduce_hbm,
    down_expand_hbm, gate_hbm, up_hbm, gate_send, gate_keep, up_send, up_keep,
    gate_scales, up_scales, tokens_ref, gradient_ref, gate_reduce_ref, up_reduce_ref, down_expand_ref, gate_ref, up_ref, sums_ref, small, sems,
):
    small_copies = fetch_all(
        [gate_scales_hbm, tokens_hbm, up_scales_hbm, gradient_hbm, gate_reduce_hbm, up_reduce_hbm, down_expand_hbm],
        [gate_scales, tokens_ref, up_scales, gradient_ref, gate_reduce_ref, up_reduce_ref, down_expand_ref],
        small,
    )
    gate_parts = start_parts(gate_hbm, gate_ref, sems.at[0], 1, FIRST_PARTS)
    up_parts = start_parts(up_hbm, up_ref, sems.at[1], 1, LATER_PARTS)
    for copy in small_copies[:3]:
        copy.wait()
    for parts, values_ref, scales_ref, send_ref, keep_ref in (
        (gate_parts, gate_ref, gate_scales, gate_send, gate_keep),
        (up_parts, up_ref, up_scales, up_send, up_keep),
    ):
        for copy, first, size in parts:
            copy.wait()
            for start in range(first, first + size, CHUNK):
                part = slice(start, start + CHUNK)
                weight = dequantize_wide(values_ref[:, part], scales_ref, start // BLOCK)
                sums_ref[part] = dot(tokens_ref[...], weight, 1, 0).T
        split_by_core(where_ref[0], sums_ref, send_ref, keep_ref)
    for copy in small_copies[3:]:
        copy.wait()
    rank = gate_reduce_ref.shape[0]
    chips, rows = gate_keep.shape[0], 3 * rank // 2
    low = jnp.concatenate(
        [
            dot(gate_reduce_ref[...], tokens_ref[...], 1, 1),
            dot(up_reduce_ref[...], tokens_ref[...], 1, 1),
            dot(down_expand_ref[...], gradient_ref[...], 1, 1),
        ],
        axis=0,
    ).astype(BF16)
    for out_ref in (up_send, up_keep):
        for block in range(2):
            out_ref[chips + block, :rows] = low[block * rows : (block + 1) * rows]
            out_ref[chips + block, rows:] = jnp.zeros_like(out_ref[chips + block, rows:])


def tall_kernel(
    where_ref, scales_hbm, gradient_hbm, values_hbm, after_ref, send_ref, keep_ref,
    scales_ref, gradient_ref, values_ref, sums_ref, small, sems,
):
    small_copies = fetch_all([scales_hbm, gradient_hbm], [scales_ref, gradient_ref], small)
    parts = start_parts(values_hbm, values_ref, sems, 0, FIRST_PARTS)
    for copy in small_copies:
        copy.wait()
    for copy, first, size in parts:
        copy.wait()
        for start in range(first, first + size, CHUNK):
            part = slice(start, start + CHUNK)
            weight = dequantize_tall(values_ref[part], scales_ref, start // BLOCK)
            sums_ref[part] = dot(weight, gradient_ref[...], 1, 1)
    split_by_core(where_ref[0], sums_ref, send_ref, keep_ref)


def wide_sums(where, gate_scales, up_scales, tokens, gradient, gate_reduce, up_reduce, down_expand, gate, up, piece):
    width, hidden = gate.shape
    chips, count = hidden // (2 * piece), tokens.shape[0]
    vmem, hbm = pl.BlockSpec(memory_space=pltpu.VMEM), pl.BlockSpec(memory_space=pltpu.HBM)
    fetched = (tokens, gradient, gate_reduce, up_reduce, down_expand, gate, up)
    return pl.pallas_call(
        wide_kernel,
        in_specs=[smem()] + [hbm] * 9,
        out_specs=[vmem] * 4,
        out_shape=[jax.ShapeDtypeStruct((chips, piece, count), BF16)] * 2
        + [jax.ShapeDtypeStruct((chips + 2, piece, count), BF16)] * 2,
        scratch_shapes=[pltpu.SMEM(gate_scales.shape, F32)] * 2
        + [pltpu.VMEM(value.shape, BF16) for value in fetched]
        + [
            pltpu.VMEM((hidden, count), F32),
            pltpu.SemaphoreType.DMA((7,)),
            pltpu.SemaphoreType.DMA((2, len(FIRST_PARTS))),
        ],
        compiler_params=params(),
    )(where, *[stay(value) for value in (gate_scales, up_scales, *fetched)])


def tall_sums(where, scales, gradient, values, piece, after):
    hidden, width = values.shape
    chips, count = hidden // (2 * piece), gradient.shape[0]
    vmem, hbm = pl.BlockSpec(memory_space=pltpu.VMEM), pl.BlockSpec(memory_space=pltpu.HBM)
    return pl.pallas_call(
        tall_kernel,
        in_specs=[smem(), hbm, hbm, hbm, pl.BlockSpec(memory_space=pl.ANY)],
        out_specs=[vmem] * 2,
        out_shape=[jax.ShapeDtypeStruct((chips, piece, count), BF16)] * 2,
        scratch_shapes=[
            pltpu.SMEM(scales.shape, F32),
            pltpu.VMEM(gradient.shape, BF16),
            pltpu.VMEM(values.shape, BF16),
            pltpu.VMEM((hidden, count), F32),
            pltpu.SemaphoreType.DMA((2,)),
            pltpu.SemaphoreType.DMA((len(FIRST_PARTS),)),
        ],
        compiler_params=params(),
    )(where, stay(scales), stay(gradient), stay(values), after)


def weights_kernel(
    gate_scales, up_scales, gate_ref, up_ref, gate_expand, up_expand, down_reduce, after_ref, gate_out, up_out, expand_ref
):
    @pl.when(pl.program_id(0) == 0)
    def _():
        for kind, ref in enumerate((gate_expand, up_expand, down_reduce)):
            expand_ref[kind] = ref[...]

    first = pl.program_id(0) * (gate_ref.shape[1] // BLOCK)
    gate_out[...] = dequantize_wide(gate_ref[...], gate_scales, first)
    up_out[...] = dequantize_wide(up_ref[...], up_scales, first)


def weights(gate_scales, up_scales, gate, up, expands, after):
    width, hidden = gate.shape
    small = expands[0].shape
    block = pl.BlockSpec((width, hidden // STEPS), lambda i: (0, i))
    return pl.pallas_call(
        weights_kernel,
        grid=(STEPS,),
        in_specs=[smem(), smem(), block, block] + [whole(small)] * 3 + [pl.BlockSpec(memory_space=pl.ANY)],
        out_specs=[block] * 2 + [whole((3,) + small)],
        out_shape=[jax.ShapeDtypeStruct(gate.shape, BF16)] * 2 + [jax.ShapeDtypeStruct((3,) + small, BF16)],
        compiler_params=params(),
        cost_estimate=pl.CostEstimate(
            flops=2 * width * hidden, bytes_accessed=8 * width * hidden, transcendentals=0
        ),
    )(gate_scales, up_scales, gate, up, *expands, after)


def vmem_call(kernel, out_shape, *args, scratch=(), unread=0):
    vmem = pl.BlockSpec(memory_space=pltpu.VMEM)
    return pl.pallas_call(
        kernel,
        in_specs=[smem()] + [vmem] * (len(args) - 1 - unread) + [pl.BlockSpec(memory_space=pl.ANY)] * unread,
        out_specs=[vmem] * len(out_shape),
        out_shape=out_shape,
        scratch_shapes=scratch,
        compiler_params=params(),
    )(*args)


def chip_of(core, first, z, second):
    return jnp.where(core == 0, first * 8 + z * 4 + second, second * 8 + z * 4 + first)


def pack_rows(where_ref, keeps, received, there, step):
    parts = []
    for near in range(2):
        chip = chip_of(where_ref[0], there, near, lax.rem(where_ref[4] + step, 4))
        parts += [keep[chip].astype(F32) + got[chip].astype(F32) for keep, got in zip(keeps, received)]
    return jnp.concatenate(parts, axis=0)


def pack_low(keep_ref, received_ref, rows):
    blocks = keep_ref.shape[0] - 2
    return jnp.concatenate(
        [keep_ref[blocks + i, :rows].astype(F32) + received_ref[blocks + i, :rows].astype(F32) for i in range(2)],
        axis=0,
    )


def halves_kernel(kinds, where_ref, *refs):
    keeps, received, outs = refs[:kinds], refs[kinds : 2 * kinds], refs[-4:]
    place = where_ref[3]
    near, far = place ^ 1, 3 - place
    pair = 2 * kinds * keeps[0].shape[1]
    for out_ref, places, steps in (
        (outs[0], (near, 3 - near), (0, 1)),
        (outs[1], (far, far ^ 1), (2, 3)),
        (outs[2], (place, far), (0, 1)),
        (outs[3], (place, near), (2, 3)),
    ):
        for i, there in enumerate(places):
            for j, step in enumerate(steps):
                rows = pack_rows(where_ref, keeps, received, there, step)
                first = (2 * i + j) * pair
                out_ref[first : first + pair] = rows.astype(out_ref.dtype)
        low_rows = out_ref.shape[0] - 4 * pair
        if low_rows:
            out_ref[4 * pair :] = pack_low(keeps[-1], received[-1], low_rows // 2).astype(out_ref.dtype)


def halves(where, keeps, received, low_rows=0, after=()):
    chips, piece, tokens = keeps[0].shape
    rows = 8 * len(keeps) * piece
    out_shape = [
        jax.ShapeDtypeStruct((rows + low_rows, tokens), BF16),
        jax.ShapeDtypeStruct((rows, tokens), BF16),
        jax.ShapeDtypeStruct((rows + low_rows, tokens), F32),
        jax.ShapeDtypeStruct((rows, tokens), F32),
    ]
    kernel = functools.partial(halves_kernel, len(keeps))
    return vmem_call(kernel, out_shape, where, *keeps, *received, *after, unread=len(after))


def add_kernel(low_rows, where_ref, one_own, two_own, one_got, two_got, one_send, two_send, one_keep, two_keep):
    for own, got, send, keep, low in (
        (one_own, one_got, one_send, one_keep, low_rows),
        (two_own, two_got, two_send, two_keep, 0),
    ):
        half = keep.shape[0] - low
        summed = own[...] + got[...].astype(F32)
        keep[:half] = summed[:half]
        send[:half] = summed[half : 2 * half].astype(BF16)
        if low:
            keep[half:] = summed[2 * half :]
            send[half:] = summed[2 * half :].astype(BF16)


def add(where, own, got, low_rows=0):
    rows, tokens = own[1].shape
    out_shape = [jax.ShapeDtypeStruct((rows // 2 + low, tokens), BF16) for low in (low_rows, 0)]
    out_shape += [jax.ShapeDtypeStruct((rows // 2 + low, tokens), F32) for low in (low_rows, 0)]
    return vmem_call(functools.partial(add_kernel, low_rows), out_shape, where, *own, *got)


def second_kernel(where_ref, *refs):
    wide, tall, expand_ref, outs, expand_out = refs[:4], refs[4:8], refs[8], refs[-5:-1], refs[-1]
    expand_out[...] = expand_ref[...]
    down = tall[0].shape[0] // 2
    pair = 2 * down

    def summed(refs, half, first, count):
        rows = slice(first, first + count)
        return refs[half][rows] + refs[2 + half][rows].astype(F32)

    low = summed(wide, 0, 2 * pair, wide[0].shape[0] - 2 * pair)
    for step, out_ref in enumerate(outs):
        half, place = step // 2, step % 2
        out_ref[:pair] = summed(wide, half, place * pair, pair).astype(out_ref.dtype)
        out_ref[pair : pair + down] = summed(tall, half, place * down, down).astype(out_ref.dtype)
        out_ref[pair + down :] = low.astype(out_ref.dtype)


def second(where, wide, tall, expand, piece, low_rows, ready):
    tokens = wide[0].shape[1]
    rows = 6 * piece + low_rows
    out_shape = [jax.ShapeDtypeStruct((rows, tokens), F32 if i == 0 else BF16) for i in range(4)]
    out_shape.append(jax.ShapeDtypeStruct(expand.shape, BF16))
    return vmem_call(second_kernel, out_shape, where, *wide, *tall, expand, *ready, unread=len(ready))


def third_kernel(where_ref, own_ref, one_ref, two_ref, three_ref, after_ref, keep_ref, send_ref):
    arrived = one_ref[...].astype(F32) + two_ref[...].astype(F32) + three_ref[...].astype(F32)
    everything = own_ref[...] + arrived
    keep_ref[...] = everything
    send_ref[...] = everything.astype(BF16)


def third(where, own, arrived, after):
    out_shape = [jax.ShapeDtypeStruct(own.shape, F32), jax.ShapeDtypeStruct(own.shape, BF16)]
    return vmem_call(third_kernel, out_shape, where, own, *arrived, after, unread=1)


def middle_kernel(
    where_ref, own_ref, arrived_ref, expand_ref, far_expand_ref,
    send_ref, keep_ref, gate_out, up_out, down_out, expands_ref, grads_ref, ranks_ref,
):
    core, z = where_ref[0], where_ref[2]
    _, rank, piece = expand_ref.shape
    half = rank // 2
    sums = own_ref[...] + arrived_ref[...].astype(F32)
    expands_ref[z] = expand_ref[...]
    expands_ref[1 - z] = far_expand_ref[...]
    lows = [sums[6 * piece + k * rank : 6 * piece + (k + 1) * rank].astype(BF16) for k in range(3)]
    keeps, sends, ranks = [], [], [0.0] * 3
    for chip in range(2):
        starts = (2 * piece * chip, 2 * piece * chip + piece, 4 * piece + piece * chip)
        gate, upper, back = [
            sums[start : start + piece] + SCALE * dot(expands_ref[chip, kind], lows[kind], 0, 0)
            for kind, start in enumerate(starts)
        ]
        sigma = jax.nn.sigmoid(gate)
        activated = gate * sigma
        hidden = activated * upper
        grad_gate = back * upper * sigma * (1.0 + gate * (1.0 - sigma))
        grad_upper = back * activated
        keeps.append(jnp.where(core == 0, grad_gate, grad_upper))
        sends.append(jnp.where(core == 0, grad_upper, grad_gate))
        for kind, grad in enumerate((grad_gate, grad_upper, hidden)):
            grads_ref[chip, kind] = grad.astype(BF16)
            ranks[kind] = ranks[kind] + dot(expands_ref[chip, kind], grads_ref[chip, kind], 1, 0)
    for kind in range(3):
        ranks_ref[kind] = ranks[kind]
    mine = pl.multiple_of(core * half, half)
    theirs = pl.multiple_of((1 - core) * half, half)
    keeps += [ranks_ref[kind, pl.ds(mine, half), :] for kind in range(3)]
    sends += [ranks_ref[kind, pl.ds(theirs, half), :] for kind in range(3)]
    keep_ref[...] = jnp.concatenate(keeps, axis=0)
    send_ref[...] = jnp.concatenate(sends, axis=0).astype(BF16)
    for kind, out_ref in enumerate((gate_out, up_out, down_out)):
        out_ref[...] = SCALE * dot(lows[kind], grads_ref[z, kind], 1, 1)


def middle(where, own, arrived, expand, far_expand):
    _, rank, piece = expand.shape
    tokens = own.shape[1]
    rows = 2 * piece + 3 * rank // 2
    out_shape = [
        jax.ShapeDtypeStruct((rows, tokens), BF16),
        jax.ShapeDtypeStruct((rows, tokens), F32),
    ] + [jax.ShapeDtypeStruct((rank, piece), F32)] * 3
    scratch = [
        pltpu.VMEM((2, 3, rank, piece), BF16),
        pltpu.VMEM((2, 3, piece, tokens), BF16),
        pltpu.VMEM((3, rank, tokens), F32),
    ]
    return vmem_call(middle_kernel, out_shape, where, own, arrived, expand, far_expand, scratch=scratch)


def pair_kernel(piece, where_ref, keep_ref, arrived_ref, out_ref):
    first = where_ref[0] == 0
    kept, arrived = keep_ref[...], arrived_ref[...].astype(F32)
    rows = []
    for chip in range(2):
        here = slice(chip * piece, (chip + 1) * piece)
        rows.append(jnp.where(first, kept[here], arrived[here]))
        rows.append(jnp.where(first, arrived[here], kept[here]))
    rows.append(kept[2 * piece :] + arrived[2 * piece :])
    out_ref[...] = jnp.concatenate(rows, axis=0).astype(BF16)


def pair_block(where, keep, arrived, piece):
    rows, tokens = keep.shape
    out_shape = [jax.ShapeDtypeStruct((rows + 2 * piece, tokens), BF16)]
    return vmem_call(functools.partial(pair_kernel, piece), out_shape, where, keep, arrived)[0]


def join_kernel(slot, where_ref, own_ref, *refs):
    arrived, out_ref = refs[:-1], refs[-1]
    count = len(refs)
    unit = (out_ref.shape[0] - own_ref.shape[0]) // (count - 1)
    place = where_ref[slot]
    rank = own_ref[unit:].astype(F32)
    for offset, ref in zip(PIECES, [own_ref, *arrived]):
        start = pl.multiple_of(lax.rem(place + count - offset, count) * unit, 16)
        out_ref[pl.ds(start, unit), :] = ref[:unit]
        if offset:
            rank = rank + ref[unit:].astype(F32)
    out_ref[count * unit :] = rank.astype(BF16)


def join(slot, where, own, arrived, rank_rows):
    rows, tokens = own.shape
    out_shape = [jax.ShapeDtypeStruct((rows + len(arrived) * (rows - rank_rows), tokens), BF16)]
    return vmem_call(functools.partial(join_kernel, slot), out_shape, where, own, *arrived)[0]


def back_kernel(last, *refs):
    if last:
        (where_ref, *pieces, gate_ref, up_ref, before_ref, rank_ref,
         keep_ref, send_ref, grads_ref, total_ref, turned_ref) = refs
    else:
        where_ref, *pieces, gate_ref, up_ref, total_ref, rank_ref, grads_ref = refs
    core = 1 - where_ref[0] if last else where_ref[0]
    place = where_ref[4] if last else where_ref[3]
    part = grads_ref.shape[0] // 4
    unit = part // 8
    for offset, ref in zip(PIECES, pieces):
        there = lax.rem(place + 4 - offset, 4)
        for other in range(4):
            for z in range(2):
                chip = chip_of(core, there, z, other)
                source = (other * 2 + z) * unit
                grads_ref[pl.ds(pl.multiple_of(chip * unit, 16), unit), :] = ref[source : source + unit]

    for turn, weight_ref in enumerate((gate_ref, up_ref)):

        @pl.when(core == turn)
        def _():
            product = dot(weight_ref[...], grads_ref[...], 1, 0)
            total_ref[...] = product + before_ref[...] if last else product

    rank = pieces[0][part:].astype(F32)
    for ref in pieces[1:]:
        rank = rank + ref[part:].astype(F32)
    if last:
        half = rank.shape[0] // 3
        ranks = []
        for kind in range(3):
            rows = slice(kind * half, (kind + 1) * half)
            ranks.append(jnp.where(core == 0, rank[rows], rank_ref[rows]))
            ranks.append(jnp.where(core == 0, rank_ref[rows], rank[rows]))
        turned_ref[...] = total_ref[...].T
        share = turned_ref.shape[0] // 4
        column = where_ref[1]
        for base, out_ref in ((column, keep_ref), (column ^ 1, send_ref)):
            rows = []
            for place in (base, 3 - base):
                piece = turned_ref[pl.ds(pl.multiple_of(place * share, share), share), :]
                rows += [piece[:, :BLOCK], piece[:, BLOCK:]]
            out_ref[...] = jnp.concatenate([*rows, *ranks], axis=0).astype(BF16)
    else:
        rank_ref[...] = rank


def back(last, where, pieces, gate_weight, up_weight, before=()):
    width, hidden = gate_weight.shape
    rows, tokens = pieces[0].shape
    rank_rows = rows - hidden // 4
    scratch = [pltpu.VMEM((hidden, tokens), BF16)]
    if last:
        out_shape = [jax.ShapeDtypeStruct((tokens // 2 * width // BLOCK + 2 * rank_rows, tokens), BF16)] * 2
        scratch += [pltpu.VMEM((width, tokens), F32), pltpu.VMEM((tokens, width), F32)]
    else:
        out_shape = [
            jax.ShapeDtypeStruct((width, tokens), F32),
            jax.ShapeDtypeStruct((rank_rows, tokens), F32),
        ]
    return vmem_call(
        functools.partial(back_kernel, last), out_shape, where, *pieces, gate_weight, up_weight, *before,
        scratch=scratch,
    )


def halfway_kernel(where_ref, own_ref, arrived_ref, main_ref, send_ref):
    rows = main_ref.shape[0]
    summed = own_ref[...].astype(F32) + arrived_ref[...].astype(F32)
    main_ref[...] = summed[:rows]
    send_ref[...] = summed[rows:].astype(BF16)


def halfway(where, own, arrived, main_rows):
    rows, tokens = own.shape
    out_shape = [
        jax.ShapeDtypeStruct((main_rows, tokens), F32),
        jax.ShapeDtypeStruct((rows - main_rows, tokens), BF16),
    ]
    return vmem_call(halfway_kernel, out_shape, where, own, arrived)


def last_kernel(
    where_ref, main_ref, own_ref, arrived_ref, tokens_ref, gradient_ref, gate_reduce_ref, up_reduce_ref,
    input_out, gate_out, up_out, down_out, wide_ref,
):
    share = input_out.shape[0]
    rank = gate_out.shape[0]
    main = main_ref[...] + arrived_ref[: 2 * share].astype(F32)
    summed = own_ref[2 * share :].astype(F32) + arrived_ref[2 * share :].astype(F32)
    sums = [summed[k * rank : (k + 1) * rank].astype(BF16) for k in range(3)]
    wide_ref[...] = dot(sums[0], gate_reduce_ref[...], 0, 0) + dot(sums[1], up_reduce_ref[...], 0, 0)
    start = pl.multiple_of(where_ref[1] * share, share)
    main = jnp.concatenate([main[:share], main[share:]], axis=1)
    input_out[...] = (main + SCALE * wide_ref[pl.ds(start, share), :]).astype(BF16)
    gate_out[...] = SCALE * dot(sums[0], tokens_ref[...], 1, 0)
    up_out[...] = SCALE * dot(sums[1], tokens_ref[...], 1, 0)
    down_out[...] = SCALE * dot(sums[2], gradient_ref[...], 1, 0)


def finish(where, main, own, arrived, tokens, gradient, gate_reduce, up_reduce):
    rank, width = gate_reduce.shape
    count = tokens.shape[0]
    out_shape = [jax.ShapeDtypeStruct((count // 4, width), BF16)] + [jax.ShapeDtypeStruct((rank, width), F32)] * 3
    return vmem_call(
        last_kernel, out_shape, where, main, own, arrived, tokens, gradient, gate_reduce, up_reduce,
        scratch=[pltpu.VMEM((count, width), F32)],
    )


def per_device(
    tokens,
    output_gradient,
    gate_values,
    gate_scales,
    up_values,
    up_scales,
    down_values,
    down_scales,
    gate_reduce_factor,
    gate_expand,
    up_reduce_factor,
    up_expand,
    down_reduce,
    down_expand,
):
    piece = gate_expand.shape[1]
    position = lax.axis_index("row")
    core, y, z, x = position & 1, (position >> 1) & 3, (position >> 3) & 1, position >> 4
    first, second_place = jnp.where(core == 0, x, y), jnp.where(core == 0, y, x)
    where = jnp.stack([core, lax.axis_index("col"), z, first, second_place]).astype(jnp.int32)

    def exchange(value):
        return lax.ppermute(value, "row", [(i, i ^ 1) for i in range(64)])

    def along_z(value):
        return lax.ppermute(value, "row", [(i, i ^ 8) for i in range(64)])

    def along(second_axis, offset, value):
        pairs = []
        for i in range(64):
            if (i % 2 == 0) != second_axis:
                pairs.append((i, (i + 16 * offset) % 64))
            else:
                pairs.append((i, i - (i // 2 % 4) * 2 + ((i // 2 + offset) % 4) * 2))
        return lax.ppermute(value, "row", pairs)

    def across(other, value):
        return lax.ppermute(value, "row", [(i, i ^ (other * (16 if i % 2 == 0 else 2))) for i in range(64)])

    def along_all(second_axis, values, order=(2, 1, 3)):
        return [along(second_axis, offset, values[offset - 1]) for offset in order]

    low_rows = 3 * gate_expand.shape[0]
    gate_send, gate_keep, up_send, up_keep = wide_sums(
        where, gate_scales, up_scales, tokens, output_gradient, gate_reduce_factor, up_reduce_factor, down_expand,
        gate_values, up_values, piece,
    )
    down_send, down_keep = tall_sums(where, down_scales.T, output_gradient, down_values, piece, gate_keep)
    keeps, received = [gate_keep, up_keep], [exchange(gate_send), exchange(up_send)]
    one, two, *wide = halves(where, keeps, received, low_rows)
    wide_got = [across(1, one), across(3, two)]
    keeps, received = [down_keep], [exchange(down_send)]
    one, two, *tall = halves(where, keeps, received, after=wide[:1])
    tall_got = [across(1, one), across(3, two)]
    gate_weight, up_weight, expand = weights(
        gate_scales, up_scales, gate_values, up_values, (gate_expand, up_expand, down_reduce), tall[0]
    )
    one, two, *wide = add(where, wide, wide_got, low_rows)
    wide += [across(3, one), across(1, two)]
    one, two, *tall = add(where, tall, tall_got)
    tall += [across(3, one), across(1, two)]
    own, *out, leaving = second(where, wide, tall, expand, piece, low_rows, (gate_weight, up_weight))
    far_expand = along_z(leaving)
    own, out = third(where, own, along_all(True, out), far_expand)
    send, keep, gate_expand_gradient, up_expand_gradient, down_reduce_gradient = middle(
        where, own, along_z(out), expand, far_expand
    )
    rank_rows = low_rows // 2
    block = pair_block(where, keep, exchange(send), piece)
    block = join(4, where, block, along_all(True, [block] * 3, PIECES[1:]), rank_rows)
    mine = [block, *along_all(False, [block] * 3, PIECES[1:])]
    theirs = [exchange(value) for value in mine]
    begun = back(False, where, mine, gate_weight, up_weight)
    own, out = back(True, where, theirs, gate_weight, up_weight, begun)
    main, out = halfway(
        where, own, lax.ppermute(out, "col", [(i, i ^ 1) for i in range(4)]), tokens.size // 4 // BLOCK
    )
    arrived = lax.ppermute(out, "col", [(i, 3 - i) for i in range(4)])
    input_gradient, gate_reduce_gradient, up_reduce_gradient, down_expand_gradient = finish(
        where, main, out, arrived, tokens, output_gradient, gate_reduce_factor, up_reduce_factor
    )
    return (
        input_gradient,
        gate_reduce_gradient,
        gate_expand_gradient,
        up_reduce_gradient,
        up_expand_gradient,
        down_reduce_gradient,
        down_expand_gradient,
    )


def solution(mesh):
    in_specs = (
        P(None, "row"),
        P(None, "row"),
        P("row", "col"),
        P("row", "col"),
        P("row", "col"),
        P("row", "col"),
        P("col", "row"),
        P("col", "row"),
        P(None, "row"),
        P(None, ("col", "row")),
        P(None, "row"),
        P(None, ("col", "row")),
        P(None, ("col", "row")),
        P(None, "row"),
    )
    out_specs = (
        P("col", "row"),
        P(None, "row"),
        P(None, ("col", "row")),
        P(None, "row"),
        P(None, ("col", "row")),
        P(None, ("col", "row")),
        P(None, "row"),
    )
    return jax.shard_map(
        per_device, mesh=mesh, in_specs=in_specs, out_specs=out_specs, check_vma=False
    )
```

```python
import functools

import jax
import jax.numpy as jnp
from jax import lax
from jax.experimental import pallas as pl
from jax.experimental.pallas import tpu as pltpu
from jax.sharding import PartitionSpec as P

BLOCK = 128
SCALE = 0.5
STEPS = 4
BF16 = jnp.bfloat16
F32 = jnp.float32
LIMIT = 32 * 1024 * 1024
CHUNK = 512
FIRST_PARTS = (1024, 2048, 3584)
LATER_PARTS = (6656,)
PIECES = (0, 1, 3, 2)


def params():
    return pltpu.CompilerParams(vmem_limit_bytes=LIMIT)


def dot(left, right, left_dim, right_dim):
    return lax.dot_general(
        left, right, (((left_dim,), (right_dim,)), ((), ())), preferred_element_type=F32
    )


def whole(shape):
    return pl.BlockSpec(shape, lambda *_: (0,) * len(shape))


def smem():
    return pl.BlockSpec(memory_space=pltpu.SMEM)


def dequantize_wide(values, scales_ref, first):
    columns = []
    for block in range(values.shape[1] // BLOCK):
        columns.append(
            jnp.concatenate(
                [
                    (values[part * BLOCK : (part + 1) * BLOCK, block * BLOCK : (block + 1) * BLOCK].astype(F32)
                     * scales_ref[part, first + block]).astype(BF16)
                    for part in range(values.shape[0] // BLOCK)
                ],
                axis=0,
            )
        )
    return jnp.concatenate(columns, axis=1)


def dequantize_tall(values, scales_ref, first):
    rows = []
    for block in range(values.shape[0] // BLOCK):
        rows.append(
            jnp.concatenate(
                [
                    (values[block * BLOCK : (block + 1) * BLOCK, part * BLOCK : (part + 1) * BLOCK].astype(F32)
                     * scales_ref[part, first + block]).astype(BF16)
                    for part in range(values.shape[1] // BLOCK)
                ],
                axis=1,
            )
        )
    return jnp.concatenate(rows, axis=0)


def split_by_core(core, sums_ref, send_ref, keep_ref):
    piece = send_ref.shape[1]
    for chip in range(sums_ref.shape[0] // (2 * piece)):
        start = chip * 2 * piece
        mine = pl.multiple_of(start + core * piece, 8)
        theirs = pl.multiple_of(start + (1 - core) * piece, 8)
        keep_ref[chip] = sums_ref[pl.ds(mine, piece), :].astype(BF16)
        send_ref[chip] = sums_ref[pl.ds(theirs, piece), :].astype(BF16)


def stay(value):
    return pltpu.with_memory_space_constraint(value, pltpu.HBM)


def fetch_all(sources, buffers, sems):
    copies = [pltpu.make_async_copy(s, b, sems.at[i]) for i, (s, b) in enumerate(zip(sources, buffers))]
    for copy in copies:
        copy.start()
    return copies


def start_parts(values_ref, buffer_ref, sems, axis, sizes):
    parts, first = [], 0
    for step, size in enumerate(sizes):
        part = pl.ds(first, size)
        place = (part, slice(None)) if axis == 0 else (slice(None), part)
        copy = pltpu.make_async_copy(values_ref.at[place], buffer_ref.at[place], sems.at[step])
        copy.start()
        parts.append((copy, first, size))
        first += size
    return parts


def wide_kernel(
    where_ref, gate_scales_hbm, up_scales_hbm, tokens_hbm, gradient_hbm, gate_reduce_hbm, up_reduce_hbm,
    down_expand_hbm, gate_hbm, up_hbm, gate_send, gate_keep, up_send, up_keep,
    gate_scales, up_scales, tokens_ref, gradient_ref, gate_reduce_ref, up_reduce_ref, down_expand_ref, gate_ref, up_ref, sums_ref, small, sems,
):
    small_copies = fetch_all(
        [gate_scales_hbm, tokens_hbm, up_scales_hbm, gradient_hbm, gate_reduce_hbm, up_reduce_hbm, down_expand_hbm],
        [gate_scales, tokens_ref, up_scales, gradient_ref, gate_reduce_ref, up_reduce_ref, down_expand_ref],
        small,
    )
    gate_parts = start_parts(gate_hbm, gate_ref, sems.at[0], 1, FIRST_PARTS)
    up_parts = start_parts(up_hbm, up_ref, sems.at[1], 1, LATER_PARTS)
    for copy in small_copies[:3]:
        copy.wait()
    for parts, values_ref, scales_ref, send_ref, keep_ref in (
        (gate_parts, gate_ref, gate_scales, gate_send, gate_keep),
        (up_parts, up_ref, up_scales, up_send, up_keep),
    ):
        for copy, first, size in parts:
            copy.wait()
            for start in range(first, first + size, CHUNK):
                part = slice(start, start + CHUNK)
                weight = dequantize_wide(values_ref[:, part], scales_ref, start // BLOCK)
                sums_ref[part] = dot(tokens_ref[...], weight, 1, 0).T
        split_by_core(where_ref[0], sums_ref, send_ref, keep_ref)
    for copy in small_copies[3:]:
        copy.wait()
    rank = gate_reduce_ref.shape[0]
    chips, rows = gate_keep.shape[0], 3 * rank // 2
    low = jnp.concatenate(
        [
            dot(gate_reduce_ref[...], tokens_ref[...], 1, 1),
            dot(up_reduce_ref[...], tokens_ref[...], 1, 1),
            dot(down_expand_ref[...], gradient_ref[...], 1, 1),
        ],
        axis=0,
    ).astype(BF16)
    for out_ref in (up_send, up_keep):
        for block in range(2):
            out_ref[chips + block, :rows] = low[block * rows : (block + 1) * rows]
            out_ref[chips + block, rows:] = jnp.zeros_like(out_ref[chips + block, rows:])


def tall_kernel(
    where_ref, scales_hbm, gradient_hbm, values_hbm, after_ref, send_ref, keep_ref,
    scales_ref, gradient_ref, values_ref, sums_ref, small, sems,
):
    small_copies = fetch_all([scales_hbm, gradient_hbm], [scales_ref, gradient_ref], small)
    parts = start_parts(values_hbm, values_ref, sems, 0, FIRST_PARTS)
    for copy in small_copies:
        copy.wait()
    for copy, first, size in parts:
        copy.wait()
        for start in range(first, first + size, CHUNK):
            part = slice(start, start + CHUNK)
            weight = dequantize_tall(values_ref[part], scales_ref, start // BLOCK)
            sums_ref[part] = dot(gradient_ref[...], weight, 1, 1).T
    split_by_core(where_ref[0], sums_ref, send_ref, keep_ref)


def wide_sums(where, gate_scales, up_scales, tokens, gradient, gate_reduce, up_reduce, down_expand, gate, up, piece):
    width, hidden = gate.shape
    chips, count = hidden // (2 * piece), tokens.shape[0]
    vmem, hbm = pl.BlockSpec(memory_space=pltpu.VMEM), pl.BlockSpec(memory_space=pltpu.HBM)
    fetched = (tokens, gradient, gate_reduce, up_reduce, down_expand, gate, up)
    return pl.pallas_call(
        wide_kernel,
        in_specs=[smem()] + [hbm] * 9,
        out_specs=[vmem] * 4,
        out_shape=[jax.ShapeDtypeStruct((chips, piece, count), BF16)] * 2
        + [jax.ShapeDtypeStruct((chips + 2, piece, count), BF16)] * 2,
        scratch_shapes=[pltpu.SMEM(gate_scales.shape, F32)] * 2
        + [pltpu.VMEM(value.shape, BF16) for value in fetched]
        + [
            pltpu.VMEM((hidden, count), F32),
            pltpu.SemaphoreType.DMA((7,)),
            pltpu.SemaphoreType.DMA((2, len(FIRST_PARTS))),
        ],
        compiler_params=params(),
    )(where, *[stay(value) for value in (gate_scales, up_scales, *fetched)])


def tall_sums(where, scales, gradient, values, piece, after):
    hidden, width = values.shape
    chips, count = hidden // (2 * piece), gradient.shape[0]
    vmem, hbm = pl.BlockSpec(memory_space=pltpu.VMEM), pl.BlockSpec(memory_space=pltpu.HBM)
    return pl.pallas_call(
        tall_kernel,
        in_specs=[smem(), hbm, hbm, hbm, pl.BlockSpec(memory_space=pl.ANY)],
        out_specs=[vmem] * 2,
        out_shape=[jax.ShapeDtypeStruct((chips, piece, count), BF16)] * 2,
        scratch_shapes=[
            pltpu.SMEM(scales.shape, F32),
            pltpu.VMEM(gradient.shape, BF16),
            pltpu.VMEM(values.shape, BF16),
            pltpu.VMEM((hidden, count), F32),
            pltpu.SemaphoreType.DMA((2,)),
            pltpu.SemaphoreType.DMA((len(FIRST_PARTS),)),
        ],
        compiler_params=params(),
    )(where, stay(scales), stay(gradient), stay(values), after)


def weights_kernel(
    gate_scales, up_scales, gate_ref, up_ref, gate_expand, up_expand, down_reduce, after_ref, gate_out, up_out, expand_ref
):
    @pl.when(pl.program_id(0) == 0)
    def _():
        for kind, ref in enumerate((gate_expand, up_expand, down_reduce)):
            expand_ref[kind] = ref[...]

    first = pl.program_id(0) * (gate_ref.shape[1] // BLOCK)
    gate_out[...] = dequantize_wide(gate_ref[...], gate_scales, first)
    up_out[...] = dequantize_wide(up_ref[...], up_scales, first)


def weights(gate_scales, up_scales, gate, up, expands, after):
    width, hidden = gate.shape
    small = expands[0].shape
    block = pl.BlockSpec((width, hidden // STEPS), lambda i: (0, i))
    return pl.pallas_call(
        weights_kernel,
        grid=(STEPS,),
        in_specs=[smem(), smem(), block, block] + [whole(small)] * 3 + [pl.BlockSpec(memory_space=pl.ANY)],
        out_specs=[block] * 2 + [whole((3,) + small)],
        out_shape=[jax.ShapeDtypeStruct(gate.shape, BF16)] * 2 + [jax.ShapeDtypeStruct((3,) + small, BF16)],
        compiler_params=params(),
        cost_estimate=pl.CostEstimate(
            flops=2 * width * hidden, bytes_accessed=8 * width * hidden, transcendentals=0
        ),
    )(gate_scales, up_scales, gate, up, *expands, after)


def vmem_call(kernel, out_shape, *args, scratch=(), unread=0):
    vmem = pl.BlockSpec(memory_space=pltpu.VMEM)
    return pl.pallas_call(
        kernel,
        in_specs=[smem()] + [vmem] * (len(args) - 1 - unread) + [pl.BlockSpec(memory_space=pl.ANY)] * unread,
        out_specs=[vmem] * len(out_shape),
        out_shape=out_shape,
        scratch_shapes=scratch,
        compiler_params=params(),
    )(*args)


def chip_of(core, first, z, second):
    return jnp.where(core == 0, first * 8 + z * 4 + second, second * 8 + z * 4 + first)


def pack_rows(where_ref, keeps, received, there, step):
    parts = []
    for near in range(2):
        chip = chip_of(where_ref[0], there, near, lax.rem(where_ref[4] + step, 4))
        parts += [keep[chip].astype(F32) + got[chip].astype(F32) for keep, got in zip(keeps, received)]
    return jnp.concatenate(parts, axis=0)


def pack_low(keep_ref, received_ref, rows):
    blocks = keep_ref.shape[0] - 2
    return jnp.concatenate(
        [keep_ref[blocks + i, :rows].astype(F32) + received_ref[blocks + i, :rows].astype(F32) for i in range(2)],
        axis=0,
    )


def halves_kernel(kinds, where_ref, *refs):
    keeps, received, outs = refs[:kinds], refs[kinds : 2 * kinds], refs[-4:]
    place = where_ref[3]
    near, far = place ^ 1, 3 - place
    pair = 2 * kinds * keeps[0].shape[1]
    for out_ref, places, steps in (
        (outs[0], (near, 3 - near), (0, 1)),
        (outs[1], (far, far ^ 1), (2, 3)),
        (outs[2], (place, far), (0, 1)),
        (outs[3], (place, near), (2, 3)),
    ):
        for i, there in enumerate(places):
            for j, step in enumerate(steps):
                rows = pack_rows(where_ref, keeps, received, there, step)
                first = (2 * i + j) * pair
                out_ref[first : first + pair] = rows.astype(out_ref.dtype)
        low_rows = out_ref.shape[0] - 4 * pair
        if low_rows:
            out_ref[4 * pair :] = pack_low(keeps[-1], received[-1], low_rows // 2).astype(out_ref.dtype)


def halves(where, keeps, received, low_rows=0, after=()):
    chips, piece, tokens = keeps[0].shape
    rows = 8 * len(keeps) * piece
    out_shape = [
        jax.ShapeDtypeStruct((rows + low_rows, tokens), BF16),
        jax.ShapeDtypeStruct((rows, tokens), BF16),
        jax.ShapeDtypeStruct((rows + low_rows, tokens), F32),
        jax.ShapeDtypeStruct((rows, tokens), F32),
    ]
    kernel = functools.partial(halves_kernel, len(keeps))
    return vmem_call(kernel, out_shape, where, *keeps, *received, *after, unread=len(after))


def add_kernel(low_rows, where_ref, one_own, two_own, one_got, two_got, one_send, two_send, one_keep, two_keep):
    for own, got, send, keep, low in (
        (one_own, one_got, one_send, one_keep, low_rows),
        (two_own, two_got, two_send, two_keep, 0),
    ):
        half = keep.shape[0] - low
        summed = own[...] + got[...].astype(F32)
        keep[:half] = summed[:half]
        send[:half] = summed[half : 2 * half].astype(BF16)
        if low:
            keep[half:] = summed[2 * half :]
            send[half:] = summed[2 * half :].astype(BF16)


def add(where, own, got, low_rows=0):
    rows, tokens = own[1].shape
    out_shape = [jax.ShapeDtypeStruct((rows // 2 + low, tokens), BF16) for low in (low_rows, 0)]
    out_shape += [jax.ShapeDtypeStruct((rows // 2 + low, tokens), F32) for low in (low_rows, 0)]
    return vmem_call(functools.partial(add_kernel, low_rows), out_shape, where, *own, *got)


def second_kernel(where_ref, *refs):
    wide, tall, expand_ref, outs, expand_out = refs[:4], refs[4:8], refs[8], refs[-5:-1], refs[-1]
    expand_out[...] = expand_ref[...]
    down = tall[0].shape[0] // 2
    pair = 2 * down

    def summed(refs, half, first, count):
        rows = slice(first, first + count)
        return refs[half][rows] + refs[2 + half][rows].astype(F32)

    low = summed(wide, 0, 2 * pair, wide[0].shape[0] - 2 * pair)
    for step, out_ref in enumerate(outs):
        half, place = step // 2, step % 2
        out_ref[:pair] = summed(wide, half, place * pair, pair).astype(out_ref.dtype)
        out_ref[pair : pair + down] = summed(tall, half, place * down, down).astype(out_ref.dtype)
        out_ref[pair + down :] = low.astype(out_ref.dtype)


def second(where, wide, tall, expand, piece, low_rows, ready):
    tokens = wide[0].shape[1]
    rows = 6 * piece + low_rows
    out_shape = [jax.ShapeDtypeStruct((rows, tokens), F32 if i == 0 else BF16) for i in range(4)]
    out_shape.append(jax.ShapeDtypeStruct(expand.shape, BF16))
    return vmem_call(second_kernel, out_shape, where, *wide, *tall, expand, *ready, unread=len(ready))


def third_kernel(where_ref, own_ref, one_ref, two_ref, three_ref, after_ref, keep_ref, send_ref):
    arrived = one_ref[...].astype(F32) + two_ref[...].astype(F32) + three_ref[...].astype(F32)
    everything = own_ref[...] + arrived
    keep_ref[...] = everything
    send_ref[...] = everything.astype(BF16)


def third(where, own, arrived, after):
    out_shape = [jax.ShapeDtypeStruct(own.shape, F32), jax.ShapeDtypeStruct(own.shape, BF16)]
    return vmem_call(third_kernel, out_shape, where, own, *arrived, after, unread=1)


def middle_kernel(
    where_ref, own_ref, arrived_ref, expand_ref, far_expand_ref,
    send_ref, keep_ref, gate_out, up_out, down_out, expands_ref, grads_ref, ranks_ref,
):
    core, z = where_ref[0], where_ref[2]
    _, rank, piece = expand_ref.shape
    half = rank // 2
    sums = own_ref[...] + arrived_ref[...].astype(F32)
    expands_ref[z] = expand_ref[...]
    expands_ref[1 - z] = far_expand_ref[...]
    lows = [sums[6 * piece + k * rank : 6 * piece + (k + 1) * rank].astype(BF16) for k in range(3)]
    keeps, sends, ranks = [], [], [0.0] * 3
    for chip in range(2):
        starts = (2 * piece * chip, 2 * piece * chip + piece, 4 * piece + piece * chip)
        gate, upper, back = [
            sums[start : start + piece] + SCALE * dot(expands_ref[chip, kind], lows[kind], 0, 0)
            for kind, start in enumerate(starts)
        ]
        sigma = jax.nn.sigmoid(gate)
        activated = gate * sigma
        hidden = activated * upper
        grad_gate = back * upper * sigma * (1.0 + gate * (1.0 - sigma))
        grad_upper = back * activated
        keeps.append(jnp.where(core == 0, grad_gate, grad_upper))
        sends.append(jnp.where(core == 0, grad_upper, grad_gate))
        for kind, grad in enumerate((grad_gate, grad_upper, hidden)):
            grads_ref[chip, kind] = grad.astype(BF16)
            ranks[kind] = ranks[kind] + dot(expands_ref[chip, kind], grads_ref[chip, kind], 1, 0)
    for kind in range(3):
        ranks_ref[kind] = ranks[kind]
    mine = pl.multiple_of(core * half, half)
    theirs = pl.multiple_of((1 - core) * half, half)
    keeps += [ranks_ref[kind, pl.ds(mine, half), :] for kind in range(3)]
    sends += [ranks_ref[kind, pl.ds(theirs, half), :] for kind in range(3)]
    keep_ref[...] = jnp.concatenate(keeps, axis=0)
    send_ref[...] = jnp.concatenate(sends, axis=0).astype(BF16)
    for kind, out_ref in enumerate((gate_out, up_out, down_out)):
        out_ref[...] = SCALE * dot(lows[kind], grads_ref[z, kind], 1, 1)


def middle(where, own, arrived, expand, far_expand):
    _, rank, piece = expand.shape
    tokens = own.shape[1]
    rows = 2 * piece + 3 * rank // 2
    out_shape = [
        jax.ShapeDtypeStruct((rows, tokens), BF16),
        jax.ShapeDtypeStruct((rows, tokens), F32),
    ] + [jax.ShapeDtypeStruct((rank, piece), F32)] * 3
    scratch = [
        pltpu.VMEM((2, 3, rank, piece), BF16),
        pltpu.VMEM((2, 3, piece, tokens), BF16),
        pltpu.VMEM((3, rank, tokens), F32),
    ]
    return vmem_call(middle_kernel, out_shape, where, own, arrived, expand, far_expand, scratch=scratch)


def pair_kernel(piece, where_ref, keep_ref, arrived_ref, out_ref):
    first = where_ref[0] == 0
    kept, arrived = keep_ref[...], arrived_ref[...].astype(F32)
    rows = []
    for chip in range(2):
        here = slice(chip * piece, (chip + 1) * piece)
        rows.append(jnp.where(first, kept[here], arrived[here]))
        rows.append(jnp.where(first, arrived[here], kept[here]))
    rows.append(kept[2 * piece :] + arrived[2 * piece :])
    out_ref[...] = jnp.concatenate(rows, axis=0).astype(BF16)


def pair_block(where, keep, arrived, piece):
    rows, tokens = keep.shape
    out_shape = [jax.ShapeDtypeStruct((rows + 2 * piece, tokens), BF16)]
    return vmem_call(functools.partial(pair_kernel, piece), out_shape, where, keep, arrived)[0]


def join_kernel(slot, where_ref, own_ref, *refs):
    arrived, out_ref = refs[:-1], refs[-1]
    count = len(refs)
    unit = (out_ref.shape[0] - own_ref.shape[0]) // (count - 1)
    place = where_ref[slot]
    rank = own_ref[unit:].astype(F32)
    for offset, ref in zip(PIECES, [own_ref, *arrived]):
        start = pl.multiple_of(lax.rem(place + count - offset, count) * unit, 16)
        out_ref[pl.ds(start, unit), :] = ref[:unit]
        if offset:
            rank = rank + ref[unit:].astype(F32)
    out_ref[count * unit :] = rank.astype(BF16)


def join(slot, where, own, arrived, rank_rows):
    rows, tokens = own.shape
    out_shape = [jax.ShapeDtypeStruct((rows + len(arrived) * (rows - rank_rows), tokens), BF16)]
    return vmem_call(functools.partial(join_kernel, slot), out_shape, where, own, *arrived)[0]


def back_kernel(last, *refs):
    if last:
        (where_ref, *pieces, gate_ref, up_ref, before_ref, rank_ref,
         keep_ref, send_ref, grads_ref, total_ref, turned_ref) = refs
    else:
        where_ref, *pieces, gate_ref, up_ref, total_ref, rank_ref, grads_ref = refs
    core = 1 - where_ref[0] if last else where_ref[0]
    place = where_ref[4] if last else where_ref[3]
    part = grads_ref.shape[0] // 4
    unit = part // 8
    for offset, ref in zip(PIECES, pieces):
        there = lax.rem(place + 4 - offset, 4)
        for other in range(4):
            for z in range(2):
                chip = chip_of(core, there, z, other)
                source = (other * 2 + z) * unit
                grads_ref[pl.ds(pl.multiple_of(chip * unit, 16), unit), :] = ref[source : source + unit]

    for turn, weight_ref in enumerate((gate_ref, up_ref)):

        @pl.when(core == turn)
        def _():
            product = dot(weight_ref[...], grads_ref[...], 1, 0)
            total_ref[...] = product + before_ref[...] if last else product

    rank = pieces[0][part:].astype(F32)
    for ref in pieces[1:]:
        rank = rank + ref[part:].astype(F32)
    if last:
        half = rank.shape[0] // 3
        ranks = []
        for kind in range(3):
            rows = slice(kind * half, (kind + 1) * half)
            ranks.append(jnp.where(core == 0, rank[rows], rank_ref[rows]))
            ranks.append(jnp.where(core == 0, rank_ref[rows], rank[rows]))
        turned_ref[...] = total_ref[...].T
        share = turned_ref.shape[0] // 4
        column = where_ref[1]
        for base, out_ref in ((column, keep_ref), (column ^ 1, send_ref)):
            rows = []
            for place in (base, 3 - base):
                piece = turned_ref[pl.ds(pl.multiple_of(place * share, share), share), :]
                rows += [piece[:, :BLOCK], piece[:, BLOCK:]]
            out_ref[...] = jnp.concatenate([*rows, *ranks], axis=0).astype(BF16)
    else:
        rank_ref[...] = rank


def back(last, where, pieces, gate_weight, up_weight, before=()):
    width, hidden = gate_weight.shape
    rows, tokens = pieces[0].shape
    rank_rows = rows - hidden // 4
    scratch = [pltpu.VMEM((hidden, tokens), BF16)]
    if last:
        out_shape = [jax.ShapeDtypeStruct((tokens // 2 * width // BLOCK + 2 * rank_rows, tokens), BF16)] * 2
        scratch += [pltpu.VMEM((width, tokens), F32), pltpu.VMEM((tokens, width), F32)]
    else:
        out_shape = [
            jax.ShapeDtypeStruct((width, tokens), F32),
            jax.ShapeDtypeStruct((rank_rows, tokens), F32),
        ]
    return vmem_call(
        functools.partial(back_kernel, last), out_shape, where, *pieces, gate_weight, up_weight, *before,
        scratch=scratch,
    )


def halfway_kernel(where_ref, own_ref, arrived_ref, main_ref, send_ref):
    rows = main_ref.shape[0]
    summed = own_ref[...].astype(F32) + arrived_ref[...].astype(F32)
    main_ref[...] = summed[:rows]
    send_ref[...] = summed[rows:].astype(BF16)


def halfway(where, own, arrived, main_rows):
    rows, tokens = own.shape
    out_shape = [
        jax.ShapeDtypeStruct((main_rows, tokens), F32),
        jax.ShapeDtypeStruct((rows - main_rows, tokens), BF16),
    ]
    return vmem_call(halfway_kernel, out_shape, where, own, arrived)


def last_kernel(
    where_ref, main_ref, own_ref, arrived_ref, tokens_ref, gradient_ref, gate_reduce_ref, up_reduce_ref,
    input_out, gate_out, up_out, down_out, wide_ref,
):
    share = input_out.shape[0]
    rank = gate_out.shape[0]
    main = main_ref[...] + arrived_ref[: 2 * share].astype(F32)
    summed = own_ref[2 * share :].astype(F32) + arrived_ref[2 * share :].astype(F32)
    sums = [summed[k * rank : (k + 1) * rank].astype(BF16) for k in range(3)]
    wide_ref[...] = dot(sums[0], gate_reduce_ref[...], 0, 0) + dot(sums[1], up_reduce_ref[...], 0, 0)
    start = pl.multiple_of(where_ref[1] * share, share)
    main = jnp.concatenate([main[:share], main[share:]], axis=1)
    input_out[...] = (main + SCALE * wide_ref[pl.ds(start, share), :]).astype(BF16)
    gate_out[...] = SCALE * dot(sums[0], tokens_ref[...], 1, 0)
    up_out[...] = SCALE * dot(sums[1], tokens_ref[...], 1, 0)
    down_out[...] = SCALE * dot(sums[2], gradient_ref[...], 1, 0)


def finish(where, main, own, arrived, tokens, gradient, gate_reduce, up_reduce):
    rank, width = gate_reduce.shape
    count = tokens.shape[0]
    out_shape = [jax.ShapeDtypeStruct((count // 4, width), BF16)] + [jax.ShapeDtypeStruct((rank, width), F32)] * 3
    return vmem_call(
        last_kernel, out_shape, where, main, own, arrived, tokens, gradient, gate_reduce, up_reduce,
        scratch=[pltpu.VMEM((count, width), F32)],
    )


def per_device(
    tokens,
    output_gradient,
    gate_values,
    gate_scales,
    up_values,
    up_scales,
    down_values,
    down_scales,
    gate_reduce_factor,
    gate_expand,
    up_reduce_factor,
    up_expand,
    down_reduce,
    down_expand,
):
    piece = gate_expand.shape[1]
    position = lax.axis_index("row")
    core, y, z, x = position & 1, (position >> 1) & 3, (position >> 3) & 1, position >> 4
    first, second_place = jnp.where(core == 0, x, y), jnp.where(core == 0, y, x)
    where = jnp.stack([core, lax.axis_index("col"), z, first, second_place]).astype(jnp.int32)

    def exchange(value):
        return lax.ppermute(value, "row", [(i, i ^ 1) for i in range(64)])

    def along_z(value):
        return lax.ppermute(value, "row", [(i, i ^ 8) for i in range(64)])

    def along(second_axis, offset, value):
        pairs = []
        for i in range(64):
            if (i % 2 == 0) != second_axis:
                pairs.append((i, (i + 16 * offset) % 64))
            else:
                pairs.append((i, i - (i // 2 % 4) * 2 + ((i // 2 + offset) % 4) * 2))
        return lax.ppermute(value, "row", pairs)

    def across(other, value):
        return lax.ppermute(value, "row", [(i, i ^ (other * (16 if i % 2 == 0 else 2))) for i in range(64)])

    def along_all(second_axis, values, order=(2, 1, 3)):
        return [along(second_axis, offset, values[offset - 1]) for offset in order]

    low_rows = 3 * gate_expand.shape[0]
    gate_send, gate_keep, up_send, up_keep = wide_sums(
        where, gate_scales, up_scales, tokens, output_gradient, gate_reduce_factor, up_reduce_factor, down_expand,
        gate_values, up_values, piece,
    )
    down_send, down_keep = tall_sums(where, down_scales.T, output_gradient, down_values, piece, gate_keep)
    keeps, received = [gate_keep, up_keep], [exchange(gate_send), exchange(up_send)]
    one, two, *wide = halves(where, keeps, received, low_rows)
    wide_got = [across(1, one), across(3, two)]
    keeps, received = [down_keep], [exchange(down_send)]
    one, two, *tall = halves(where, keeps, received, after=wide[:1])
    tall_got = [across(1, one), across(3, two)]
    gate_weight, up_weight, expand = weights(
        gate_scales, up_scales, gate_values, up_values, (gate_expand, up_expand, down_reduce), tall[0]
    )
    one, two, *wide = add(where, wide, wide_got, low_rows)
    wide += [across(3, one), across(1, two)]
    one, two, *tall = add(where, tall, tall_got)
    tall += [across(3, one), across(1, two)]
    own, *out, leaving = second(where, wide, tall, expand, piece, low_rows, (gate_weight, up_weight))
    far_expand = along_z(leaving)
    own, out = third(where, own, along_all(True, out), far_expand)
    send, keep, gate_expand_gradient, up_expand_gradient, down_reduce_gradient = middle(
        where, own, along_z(out), expand, far_expand
    )
    rank_rows = low_rows // 2
    block = pair_block(where, keep, exchange(send), piece)
    block = join(4, where, block, along_all(True, [block] * 3, PIECES[1:]), rank_rows)
    mine = [block, *along_all(False, [block] * 3, PIECES[1:])]
    theirs = [exchange(value) for value in mine]
    begun = back(False, where, mine, gate_weight, up_weight)
    own, out = back(True, where, theirs, gate_weight, up_weight, begun)
    main, out = halfway(
        where, own, lax.ppermute(out, "col", [(i, i ^ 1) for i in range(4)]), tokens.size // 4 // BLOCK
    )
    arrived = lax.ppermute(out, "col", [(i, 3 - i) for i in range(4)])
    input_gradient, gate_reduce_gradient, up_reduce_gradient, down_expand_gradient = finish(
        where, main, out, arrived, tokens, output_gradient, gate_reduce_factor, up_reduce_factor
    )
    return (
        input_gradient,
        gate_reduce_gradient,
        gate_expand_gradient,
        up_reduce_gradient,
        up_expand_gradient,
        down_reduce_gradient,
        down_expand_gradient,
    )


def solution(mesh):
    in_specs = (
        P(None, "row"),
        P(None, "row"),
        P("row", "col"),
        P("row", "col"),
        P("row", "col"),
        P("row", "col"),
        P("col", "row"),
        P("col", "row"),
        P(None, "row"),
        P(None, ("col", "row")),
        P(None, "row"),
        P(None, ("col", "row")),
        P(None, ("col", "row")),
        P(None, "row"),
    )
    out_specs = (
        P("col", "row"),
        P(None, "row"),
        P(None, ("col", "row")),
        P(None, "row"),
        P(None, ("col", "row")),
        P(None, ("col", "row")),
        P(None, "row"),
    )
    return jax.shard_map(
        per_device, mesh=mesh, in_specs=in_specs, out_specs=out_specs, check_vma=False
    )
```
